32 devices in a mesh: dp: 4 (over y, x), context: 8 (over z, core).
Axes of the slice: x: 2, y: 2, z: 4, core: 2. Of those that a mesh axis runs over, the one named last changes fastest.
Arguments:
- query_rows: bfloat16 [4, 1536, 1024], P('dp', 'context'), may hold values from -40 to 40
- key_rows: bfloat16 [4, 1536, 128], P('dp', 'context'), may hold values from -12 to 12
- value_rows: bfloat16 [4, 1536, 128], P('dp', 'context'), may hold values from -6 to 6
- out_grads: bfloat16 [4, 1536, 1024], P('dp', 'context'), may hold values from -16 to 16
- layer_input: bfloat16 [4, 1536, 8192], P('dp', 'context'), may hold values from -6 to 6
- doc_ids: int32 [4, 1536], P('dp'), may hold values from 0 to 7, never falling along the last dimension, each value on 1 to 768 neighbouring positions
- pair_span: int32 [8], replicated, may hold values from 0 to 7, each once
Outputs:
- grad_qkv: bfloat16 [4, 1536, 1280], P('dp', 'context')
- grad_weight: float32 [8192, 1280], P(('dp', 'context'))
- amax_record: float32 [4, 8, 2], P('dp', 'context')
The draws below stay inside these ranges and needn't reach their ends.
Inputs may be any that keep to these rules, and one draw needn't show every extreme that they name: doc_ids[b] never falls along positions; each document holds 1 to 768 positions, one exactly 768. `pair_span`: each of 0 to 7 once.
All inputs are finite; a program needn't handle non-finite values.
Results may differ from the reference program's by a relative error of at most 0.0056.
Values may be sent and summed in bfloat16 or wider, within the bound.
No kernel may reach another device: no remote copies, remote signals or barrier semaphores. Data moves between devices by JAX's collectives and lax.ppermute only.
A program may use at most 64 MiB of HBM per device.

```python
import math
import jax
import jax.numpy as jnp
import numpy as np
from jax import lax

D = 8192
H = 8
HD = 128
DOCS = 8
SPAN = 96
PAIRS = 8
LEN = 1536
SEQS = 4
QKV = 1280


def draw_query_rows(key, part):
    drawn = jax.random.truncated_normal(jax.random.fold_in(key, 3), -4.0, 4.0, (SEQS, LEN, H, HD), jnp.float32)
    return drawn.reshape(SEQS, LEN, H * HD).astype(jnp.bfloat16)


def draw_key_rows(key, part):
    drawn = jax.random.truncated_normal(jax.random.fold_in(key, 5), -4.0, 4.0, (SEQS, LEN, HD), jnp.float32)
    return drawn.astype(jnp.bfloat16)


def draw_out_grads(key, part):
    rising = jnp.arange(SEQS * LEN, dtype=jnp.float32).reshape(SEQS, LEN, 1) / (SEQS * LEN)
    noise = jax.random.truncated_normal(jax.random.fold_in(key, 9), -4.0, 4.0, (SEQS, LEN, H * HD), jnp.float32)
    factor = 3.0 ** rising
    return (noise * factor).astype(jnp.bfloat16)


def spiked(values, own_key, source, target, parts, factor):
    owner, partner = [(jnp.arange(values.shape[position]) // (values.shape[position] // parts)).reshape([-1 if axis == position else 1 for axis in range(values.ndim)]) for position in (source, target)]
    chosen = jax.random.permutation(own_key, parts)[partner]
    strong = (owner == chosen) | (owner == (partner + parts // 2) % parts)
    return jnp.where(strong, factor * values, values)


def block_scale(stream_key, dims, split, smallest, largest):
    factor_of = 1.0
    for dim, shards_of in split:
        heights = jax.random.uniform(jax.random.fold_in(jax.random.fold_in(stream_key, 6), dim), (shards_of,), jnp.float32, smallest / len(split), largest / len(split))
        factor_of = factor_of * jnp.repeat(jnp.exp(heights), dims[dim] // shards_of).reshape((-1,) + (1,) * (len(dims) - 1 - dim))
    return factor_of


def length_profile(count, total, most, skew):
    portions = [(1 << 20) // math.isqrt(rank ** skew) + 1 for rank in range(2, count + 1)]
    spare, given = total - most - (count - 1), [1] * (count - 1)
    while spare > 0:
        candidates = [i for i in range(count - 1) if given[i] < most]
        pool, left = sum([portions[i] for i in candidates]), spare
        for i in candidates:
            more = min(most - given[i], max(1, left * portions[i] // pool), spare)
            given[i] = given[i] + more
            spare = spare - more
    return np.array([most] + given)


def uneven(rng, count, total, most, skew):
    if count == 2:
        one = jax.random.randint(rng, (), max(1, total - most), min(most, total - 1) + 1)
        return jnp.stack([one, total - one])
    sizes = jnp.asarray(length_profile(count, total, most, skew), jnp.int32)
    twos = (count - 1) // 2
    donor, receiver = sizes[1:1 + 2 * twos:2], sizes[2:2 + 2 * twos:2]
    slack = jnp.minimum(donor - 1, most - receiver)
    shifted = jax.random.randint(jax.random.fold_in(rng, 1), (twos,), 0, 1 << 20) % (slack + 1)
    sizes = sizes.at[1:1 + 2 * twos:2].set(donor - shifted).at[2:2 + 2 * twos:2].set(receiver + shifted)
    return sizes[jax.random.permutation(jax.random.fold_in(rng, 2), count)]


def scatter_about(stream_key, shape, deviation, bound, split=(), kind=jnp.bfloat16):
    level = block_scale(stream_key, shape, split, -0.22, 0.18) if split else 1.0
    values = jax.random.normal(stream_key, shape, jnp.float32) * deviation * level
    return jnp.minimum(jnp.maximum(values, -bound), bound).astype(kind)


def bell_draw_with(stream_key, dims, deviation, limit, pieces, heavy, kind=jnp.bfloat16):
    drawn = deviation * jax.random.normal(stream_key, dims, jnp.float32)
    if pieces:
        drawn = drawn * block_scale(stream_key, dims, pieces, -0.22, 0.18)
    return jnp.clip(spiked(drawn, jax.random.fold_in(stream_key, 3), *heavy), -limit, limit).astype(kind)


def setup_inputs(seed: int = 0) -> dict:
    arg_keys = jax.random.split(jax.random.key(seed), 8)
    query_rows = draw_query_rows(jax.random.fold_in(arg_keys[7], 71), 0)
    key_rows = draw_key_rows(jax.random.fold_in(arg_keys[7], 71), 0)
    value_rows = scatter_about(arg_keys[2], (SEQS, LEN, HD), 1.0, 6.0, ((0, 4), (1, 8)))
    out_grads = draw_out_grads(jax.random.fold_in(arg_keys[7], 71), 0)
    layer_input = bell_draw_with(arg_keys[4], (SEQS, LEN, D), 1.0, 6.0, ((0, 4), (1, 8)), (1, 2, 8, 2.0))
    doc_ids = jax.vmap(lambda own: jnp.searchsorted(jnp.cumsum(uneven(own, DOCS, LEN, LEN // 2, 2)), jnp.arange(LEN), side="right"))(jax.random.split(arg_keys[5], SEQS)).reshape((SEQS, LEN)).astype(jnp.int32)
    pair_span = jax.random.permutation(arg_keys[6], PAIRS).astype(jnp.int32)
    return dict(query_rows=query_rows, key_rows=key_rows, value_rows=value_rows, out_grads=out_grads, layer_input=layer_input, doc_ids=doc_ids, pair_span=pair_span)


THETA_BASE = 500000.0

def rope_table(seq_len, head_dim):
    inverse_freq = THETA_BASE ** (-2.0 * np.arange(head_dim // 2) / head_dim)
    angles = np.arange(seq_len)[:, None] * inverse_freq[None, :]
    angles = np.concatenate([angles, angles], axis=1)
    return (np.cos(angles).astype(np.float32), np.sin(angles).astype(np.float32))

def stored_positions(pair_span, pairs, span_len):
    block_index = jnp.arange(2 * pairs, dtype=jnp.int32)
    owner_pair = pair_span[block_index // 2]
    span_index = jnp.where(block_index % 2 == 0, owner_pair, 2 * pairs - 1 - owner_pair)
    row_index = jnp.arange(2 * pairs * span_len, dtype=jnp.int32)
    return (span_index[row_index // span_len] * span_len + row_index % span_len, span_index)

def unrotate(grad_rows, cosine, sine_rows):
    half_dim = grad_rows.shape[-1] // 2
    turned = jnp.concatenate([-grad_rows[..., half_dim:], grad_rows[..., :half_dim]], axis=-1)
    return grad_rows * cosine - turned * sine_rows

def sequence_grads(query_rows, key_rows, value_rows, out_grads, seq_docs, positions, cosine, sine_rows):
    score_scale = 1.0 / math.sqrt(HD)
    query_wide = query_rows.reshape(LEN, H, HD).astype(jnp.float32)
    key_wide = key_rows.astype(jnp.float32)
    value_wide = value_rows.astype(jnp.float32)
    grad_wide = out_grads.reshape(LEN, H, HD).astype(jnp.float32)
    row_docs = seq_docs[positions]
    allowed = (positions[None, :] <= positions[:, None]) & (row_docs[None, :] == row_docs[:, None])
    scores = jnp.einsum('ihd,jd->hij', query_wide, key_wide) * score_scale
    masked = jnp.where(allowed[None], scores, -jnp.inf)
    row_top = lax.optimization_barrier(jnp.max(masked, axis=2, keepdims=True))
    weights = jnp.where(allowed[None], jnp.exp(scores - row_top), 0.0)
    prob_rows = weights / lax.optimization_barrier(jnp.sum(weights, axis=2, keepdims=True))
    dprobs = jnp.einsum('ihd,jd->hij', grad_wide, value_wide)
    row_delta = lax.optimization_barrier(jnp.sum(prob_rows * dprobs, axis=2, keepdims=True))
    dscores = prob_rows * (dprobs - row_delta)
    probs_low = lax.optimization_barrier(prob_rows.astype(jnp.bfloat16)).astype(jnp.float32)
    dscores_low = lax.optimization_barrier(dscores.astype(jnp.bfloat16)).astype(jnp.float32)
    grad_v = jnp.einsum('hij,ihd->jd', probs_low, grad_wide)
    grad_q = jnp.einsum('hij,jd->ihd', dscores_low, key_wide) * score_scale
    grad_k = jnp.einsum('hij,ihd->jd', dscores_low, query_wide) * score_scale
    grad_q = unrotate(grad_q, cosine[:, None, :], sine_rows[:, None, :])
    grad_k = unrotate(grad_k, cosine, sine_rows)
    joined = jnp.concatenate([grad_q.reshape(LEN, H * HD), grad_k, grad_v], axis=1).astype(jnp.bfloat16)
    return (joined, jnp.max(jnp.abs(dscores)))

def reference(query_rows, key_rows, value_rows, out_grads, layer_input, doc_ids, pair_span):
    positions, span_index = stored_positions(pair_span, PAIRS, SPAN)
    cos_tab, sin_tab = rope_table(LEN, HD)
    cosine = jnp.asarray(cos_tab)[positions]
    sine_rows = jnp.asarray(sin_tab)[positions]

    def per_sequence(operands):
        query_one, key_one, value_one, grad_one, docs_one = operands
        return sequence_grads(query_one, key_one, value_one, grad_one, docs_one, positions, cosine, sine_rows)
    grad_qkv, ds_maxima = lax.map(per_sequence, (query_rows, key_rows, value_rows, out_grads, doc_ids))
    grad_weight = jnp.dot(layer_input.reshape(SEQS * LEN, D).T, grad_qkv.reshape(SEQS * LEN, QKV), preferred_element_type=jnp.float32)
    out_max = jnp.max(jnp.abs(out_grads)).astype(jnp.float32)
    maxima = jnp.stack([out_max, jnp.max(ds_maxima)])
    amax_record = jnp.broadcast_to(maxima, (SEQS, PAIRS, 2))
    return (grad_qkv, grad_weight, amax_record)
```

```python
import functools
import math

import jax
import jax.numpy as jnp
import numpy as np
from jax import lax
from jax.experimental import pallas as pl
from jax.experimental.pallas import tpu as pltpu
from jax.sharding import PartitionSpec as P

THETA_BASE = 500000.0
NEG_LARGE = -1e30
DOC_VALUES = 8
EXTRA = 16
F32 = jnp.float32
BF16 = jnp.bfloat16
VMEM = pl.BlockSpec(memory_space=pltpu.VMEM)
SMEM = pl.BlockSpec(memory_space=pltpu.SMEM)
ANY = pl.BlockSpec(memory_space=pl.ANY)


def rope_tables(seq_len, head_dim):
    inverse_freq = THETA_BASE ** (-2.0 * np.arange(head_dim // 2) / head_dim)
    angles = np.arange(seq_len)[:, None] * inverse_freq[None, :]
    angles = np.concatenate([angles, angles], axis=1)
    sign = np.where(np.arange(head_dim) < head_dim // 2, 1.0, -1.0)
    return np.concatenate(
        [np.cos(angles).astype(np.float32), (np.sin(angles) * sign).astype(np.float32)], axis=1
    )


def unrotate(rows, cosine, signed_sine):
    return rows * cosine + pltpu.roll(rows, rows.shape[-1] // 2, 1) * signed_sine


def span_of(pair, half, shards):
    return pair if half == 0 else 2 * shards - 1 - pair


def spread_max(out_max, ds_max, width):
    high = ds_max.astype(BF16).astype(F32)
    middle = (ds_max - high).astype(BF16).astype(F32)
    low = ds_max - high - middle
    row = lax.broadcasted_iota(jnp.int32, (EXTRA, width), 0)
    return jnp.where(
        row == 0,
        out_max,
        jnp.where(row == 1, high, jnp.where(row == 2, middle, jnp.where(row == 3, low, 0.0))),
    )


def read_max(rows):
    wide = rows.astype(F32)
    return wide[0:1], wide[1:2] + wide[2:3] + wide[3:4]


def attend_kernel(shards, heads, pair_ref, docs_ref, rope, q_cats, g_cats, *refs):
    pieces = refs[:shards]
    (gq_ref, keep_ref, send_ref, keys, values, score_buf, dprob_buf, dq_acc, dk_acc, dv_acc, order) = refs[shards:]
    lanes, head_dim = q_cats.shape[1:]
    span_len = lanes // heads
    tok_dev = 2 * span_len
    scale = 1.0 / math.sqrt(head_dim)
    me = lax.axis_index("context")
    pair = pair_ref[me]
    for index in range(shards):
        rows = pl.ds(index * tok_dev, tok_dev)
        keys[rows] = pieces[index][:, :head_dim]
        values[rows] = pieces[index][:, head_dim:]
    dk_acc[...] = jnp.zeros_like(dk_acc)
    dv_acc[...] = jnp.zeros_like(dv_acc)
    docs = docs_ref[...]
    starts = [jnp.sum(jnp.where(docs < value, 1.0, 0.0)) for value in range(1, DOC_VALUES)]
    out_max = jnp.max(jnp.abs(g_cats[...].astype(F32)))
    ds_top = jnp.zeros((1, lanes), F32)
    lane = lax.broadcasted_iota(jnp.int32, (1, lanes), 1)
    lane_row = lane % span_len
    sub = lax.broadcasted_iota(jnp.int32, (span_len, 1), 0)

    for half in range(2):
        span = span_of(pair, half, shards)
        base = span * span_len
        base_f = base.astype(F32)
        first_start = jnp.float32(0.0)
        for start in starts:
            first_start = jnp.maximum(first_start, jnp.where(start <= base_f, start, 0.0))
        first_key = first_start.astype(jnp.int32)

        def listing(block, count):
            other = pair_ref[me ^ (block // 2)]
            key_span = jnp.where(block % 2 == 0, other, 2 * shards - 1 - other)
            order[0, count] = block
            order[1, count] = key_span
            needed = (key_span <= span) & (key_span * span_len + span_len > first_key)
            return count + needed.astype(jnp.int32)

        count = lax.fori_loop(0, 2 * shards, listing, jnp.int32(0))
        query_pos = base + lane_row
        query_f = query_pos.astype(F32)
        doc_start = jnp.zeros((1, lanes), F32)
        for start in starts:
            doc_start = jnp.maximum(doc_start, jnp.where(start <= query_f, start, 0.0))
        doc_first = doc_start.astype(jnp.int32)
        own = pl.ds(half * span_len, span_len)
        q_cat, g_cat = q_cats.at[half], g_cats.at[half]

        def score_step(index, top):
            block = order[0, index]
            key_pos = order[1, index] * span_len + sub
            rows = pl.ds(pl.multiple_of(block * span_len, span_len), span_len)
            scores = lax.dot_general(
                keys[rows], q_cat[...], (((1,), (1,)), ((), ())), preferred_element_type=F32
            )
            allowed = (key_pos <= query_pos) & (key_pos >= doc_first)
            scores = jnp.where(allowed, scores, NEG_LARGE)
            score_buf[index] = scores
            dprob_buf[index] = lax.dot_general(
                values[rows], g_cat[...], (((1,), (1,)), ((), ())), preferred_element_type=F32
            )
            return jnp.maximum(top, jnp.max(scores, axis=0, keepdims=True))

        top = lax.fori_loop(0, count, score_step, jnp.full((1, lanes), NEG_LARGE, F32))

        def exp_step(index, sums):
            total, weighted = sums
            expd = jnp.exp((score_buf[index] - top) * scale)
            score_buf[index] = expd
            return (
                total + jnp.sum(expd, axis=0, keepdims=True),
                weighted + jnp.sum(expd * dprob_buf[index], axis=0, keepdims=True),
            )

        zero_row = jnp.zeros((1, lanes), F32)
        total, weighted = lax.fori_loop(0, count, exp_step, (zero_row, zero_row))
        inverse = 1.0 / total
        delta = weighted * inverse
        dq_acc[...] = jnp.zeros_like(dq_acc)

        def grad_step(index, ds_now):
            block = order[0, index]
            rows = pl.ds(pl.multiple_of(block * span_len, span_len), span_len)
            probs = score_buf[index] * inverse
            dscores = probs * (dprob_buf[index] - delta)
            probs_low = probs.astype(BF16)
            ds_low = dscores.astype(BF16)
            dv_acc[rows] += jnp.dot(probs_low, g_cat[...], preferred_element_type=F32)
            dk_acc[rows] += jnp.dot(ds_low, q_cat[...], preferred_element_type=F32)
            dq_acc[...] += lax.dot_general(
                keys[rows], ds_low, (((0,), (0,)), ((), ())), preferred_element_type=F32
            )
            return jnp.maximum(ds_now, jnp.max(jnp.abs(dscores), axis=0, keepdims=True))

        ds_top = lax.fori_loop(0, count, grad_step, ds_top)
        cosine = rope[half, :, :head_dim]
        signed_sine = rope[half, :, head_dim:]
        grad_q = dq_acc[...].T * scale
        for head in range(heads):
            part = grad_q[head * span_len : (head + 1) * span_len]
            gq_ref[own, pl.ds(head * head_dim, head_dim)] = unrotate(part, cosine, signed_sine).astype(BF16)

    ds_max = jnp.max(ds_top)
    extra = spread_max(out_max, ds_max, 2 * head_dim)
    row = lax.broadcasted_iota(jnp.int32, (EXTRA, 2 * head_dim), 0)
    plain = jnp.where(row == 0, out_max, jnp.where(row == 1, ds_max, 0.0))
    for index in range(shards):
        rows = pl.ds(index * tok_dev, tok_dev)
        target = (keep_ref, send_ref)[index % 2]
        kind = target.dtype
        target[index // 2, :tok_dev, :head_dim] = dk_acc[rows].astype(kind)
        target[index // 2, :tok_dev, head_dim:] = dv_acc[rows].astype(kind)
        target[index // 2, tok_dev:] = (extra if index % 2 else plain).astype(kind)


def merge_kernel(keep_ref, got_ref, own_ref, *send_refs):
    tok_dev = keep_ref.shape[1] - EXTRA
    width = keep_ref.shape[2]
    out_max, ds_max = read_max(got_ref[0, tok_dev:])
    out_max = jnp.maximum(out_max, keep_ref[0, tok_dev : tok_dev + 1])
    ds_max = jnp.maximum(ds_max, keep_ref[0, tok_dev + 1 : tok_dev + 2])
    extra = spread_max(out_max, ds_max, width)
    for index in range(keep_ref.shape[0]):
        both = keep_ref[index, :tok_dev] + got_ref[index, :tok_dev].astype(F32)
        target = own_ref if index == 0 else send_refs[index - 1]
        target[:tok_dev] = both.astype(target.dtype)
        target[tok_dev:] = extra.astype(target.dtype)


def finish_kernel(rope, gq_ref, own_ref, *refs):
    got_refs, (rows_ref, gkv_ref) = refs[:-2], refs[-2:]
    tok_dev = gq_ref.shape[0]
    head_dim = own_ref.shape[1] // 2
    total = own_ref[:tok_dev]
    out_max, ds_max = read_max(own_ref[tok_dev:])
    for got_ref in got_refs:
        total = total + got_ref[:tok_dev].astype(F32)
        other_out, other_ds = read_max(got_ref[tok_dev:])
        out_max = jnp.maximum(out_max, other_out)
        ds_max = jnp.maximum(ds_max, other_ds)
    wide = rope[...].reshape(tok_dev, 2 * head_dim)
    grad_k = unrotate(
        total[:, :head_dim] * (1.0 / math.sqrt(head_dim)), wide[:, :head_dim], wide[:, head_dim:]
    ).astype(BF16)
    grad_v = total[:, head_dim:].astype(BF16)
    gkv_ref[:tok_dev, :head_dim] = grad_k
    gkv_ref[:tok_dev, head_dim:] = grad_v
    gkv_ref[tok_dev:] = spread_max(out_max, ds_max, 2 * head_dim).astype(BF16)
    width = gq_ref.shape[1]
    rows_ref[:, :width] = gq_ref[...]
    rows_ref[:, width : width + head_dim] = grad_k
    rows_ref[:, width + head_dim :] = grad_v


def partial_kernel(count, first, tile, adds, *refs):
    xs, gs = refs[:count], refs[count : 2 * count]
    rest = refs[2 * count :]
    got_ref, outs = (rest[0], rest[1:]) if adds else (None, rest)
    blocks = len(outs) if adds else outs[0].shape[0] // tile
    tok_dev = xs[0].shape[0]
    for block in range(blocks):
        cols = slice(first + block * tile, first + (block + 1) * tile)
        total = None
        for x_ref, g_ref in zip(xs, gs):
            term = lax.dot_general(
                x_ref[:, cols], g_ref[:tok_dev], (((0,), (0,)), ((), ())), preferred_element_type=F32
            )
            total = term if total is None else total + term
        rows = slice(block * tile, (block + 1) * tile)
        if adds:
            total = total + got_ref[rows].astype(F32)
            outs[block][...] = total.astype(outs[block].dtype)
        else:
            outs[0][rows] = total.astype(outs[0].dtype)


def total_kernel(groups, places, *refs):
    out_ref, amax_ref = refs[-2:]
    used = 0
    for group, (rows, cols) in zip(groups, places):
        total = refs[used][...]
        for ref in refs[used + 1 : used + group]:
            total = total + ref[...].astype(F32)
        used += group
        out_ref[rows, cols] = total
    out_max, ds_max = None, None
    for ref in refs[used:-2]:
        tok_dev = ref.shape[0] - EXTRA
        other_out, other_ds = read_max(ref[tok_dev:])
        out_max = other_out if out_max is None else jnp.maximum(out_max, other_out)
        ds_max = other_ds if ds_max is None else jnp.maximum(ds_max, other_ds)
    lane = lax.broadcasted_iota(jnp.int32, (1, 2), 1)
    amax_ref[0] = jnp.where(lane == 0, out_max[:, :2], ds_max[:, :2])


def prepare_kernel(replicas, shards, order, tile, pair_ref, table_ref, q_ref, g_ref, *refs):
    rope_sems = refs[-1]
    rope_ref, q_cat, g_cat = refs[-4:-1]
    tok_dev = q_ref.shape[0]
    span_len = tok_dev // 2
    head_dim = q_cat.shape[2]
    rep, me = lax.axis_index("dp"), lax.axis_index("context")
    copies = []
    for half in range(2):
        start = pl.multiple_of(span_of(pair_ref[me], half, shards) * span_len, 8)
        copy = pltpu.make_async_copy(table_ref.at[pl.ds(start, span_len)], rope_ref.at[half], rope_sems.at[half])
        copy.start()
        copies.append(copy)
    if len(refs) > 4:
        x_ref, outs = refs[0], refs[1:-4]
        for half in range(2):
            for step in range(replicas):
                for place, relative in enumerate(order):
                    source = (((rep ^ step) * shards + (me ^ relative)) * 2 + half) * tile
                    outs[half * replicas + step][:, place * tile : (place + 1) * tile] = x_ref[
                        :, pl.ds(pl.multiple_of(source, tile), tile)
                    ]
    for half in range(2):
        own = slice(half * span_len, (half + 1) * span_len)
        for head in range(q_ref.shape[1] // head_dim):
            rows = slice(head * span_len, (head + 1) * span_len)
            cols = slice(head * head_dim, (head + 1) * head_dim)
            q_cat[half, rows] = q_ref[own, cols]
            g_cat[half, rows] = g_ref[own, cols]
    for copy in copies:
        copy.wait()


def params(mebibytes):
    return pltpu.CompilerParams(vmem_limit_bytes=mebibytes << 20)


def cost(microseconds):
    return pl.CostEstimate(flops=int(microseconds * 1.0e9), bytes_accessed=0, transcendentals=0)


def local(query_rows, key_rows, value_rows, out_grads, layer_input, doc_ids, pair_span):
    shards = lax.axis_size("context")
    replicas = lax.axis_size("dp")
    tok_dev = query_rows.shape[1]
    head_dim = key_rows.shape[2]
    width = query_rows.shape[2]
    heads = width // head_dim
    model_width = layer_input.shape[2]
    span_len = tok_dev // 2
    seq_len = tok_dev * shards
    qkv_width = width + 2 * head_dim
    lanes = heads * span_len
    slice_rows = model_width // (replicas * shards)
    tile = slice_rows // 2
    table = jnp.asarray(rope_tables(seq_len, head_dim))
    order = list(range(1, shards, 2)) + list(range(0, shards, 2))

    def context_move(x, step):
        return lax.ppermute(x, "context", [(i, i ^ step) for i in range(shards)])

    def dp_move(x, step):
        return lax.ppermute(x, "dp", [(i, i ^ step) for i in range(replicas)])

    def struct(shape, kind=BF16):
        return jax.ShapeDtypeStruct(shape, kind)

    own_kv = jnp.concatenate([key_rows[0], value_rows[0]], axis=1)
    pieces = [None] * shards
    pieces[0] = own_kv
    for step in range(2, shards, 2):
        pieces[step] = context_move(own_kv, step)
    for step in range(0, shards, 2):
        pieces[step + 1] = context_move(pieces[step], 1)

    x_local = layer_input[0]
    rope_shape = (2, span_len, 2 * head_dim)
    cat_shape = (2, lanes, head_dim)
    prepared = pl.pallas_call(
        functools.partial(prepare_kernel, replicas, shards, order, tile),
        out_shape=[struct((tok_dev, shards * tile))] * (2 * replicas if tile % 128 == 0 else 0)
        + [struct(rope_shape, F32), struct(cat_shape), struct(cat_shape)],
        in_specs=[SMEM, ANY, VMEM, VMEM] + [VMEM] * (tile % 128 == 0),
        out_specs=[VMEM] * (3 + (2 * replicas if tile % 128 == 0 else 0)),
        scratch_shapes=[pltpu.SemaphoreType.DMA((2,))],
        compiler_params=params(40),
        cost_estimate=cost(4),
        name="prepare",
    )(pair_span, table, query_rows[0], out_grads[0], *([x_local] if tile % 128 == 0 else []))
    packed = prepared[:-3]
    rope, q_cats, g_cats = prepared[-3:]
    if tile % 128:
        me, rep = lax.axis_index("context"), lax.axis_index("dp")
        parts = []
        for step in range(replicas):
            part = lax.dynamic_slice_in_dim(x_local, (rep ^ step) * shards * slice_rows, shards * slice_rows, 1)
            part = part.reshape(tok_dev, shards, 2, tile)
            parts.append(jnp.take(part, jnp.asarray(order, jnp.int32) ^ me, axis=1))
        packed = [part[:, :, half].reshape(tok_dev, shards * tile) for half in range(2) for part in parts]
    x_halves = [list(packed[:replicas]), list(packed[replicas:])]
    x_halves[0][1:] = [dp_move(x_halves[0][step], step) for step in range(1, replicas)]

    buf = (2 * shards, span_len, lanes)
    grad_q, keep, send = pl.pallas_call(
        functools.partial(attend_kernel, shards, heads),
        out_shape=[
            struct((tok_dev, width)),
            struct((shards // 2, tok_dev + EXTRA, 2 * head_dim), F32),
            struct((shards // 2, tok_dev + EXTRA, 2 * head_dim)),
        ],
        in_specs=[SMEM, VMEM, VMEM, VMEM, VMEM] + [VMEM] * shards,
        out_specs=[VMEM] * 3,
        scratch_shapes=[
            pltpu.VMEM((seq_len, head_dim), BF16),
            pltpu.VMEM((seq_len, head_dim), BF16),
            pltpu.VMEM(buf, F32),
            pltpu.VMEM(buf, F32),
            pltpu.VMEM((head_dim, lanes), F32),
            pltpu.VMEM((seq_len, head_dim), F32),
            pltpu.VMEM((seq_len, head_dim), F32),
            pltpu.SMEM((2, 2 * shards + 1), jnp.int32),
        ],
        compiler_params=params(48),
        cost_estimate=cost(12),
        name="attend",
    )(pair_span, doc_ids, rope, q_cats, g_cats, *pieces)

    gq = [grad_q] + [dp_move(grad_q, step) for step in range(1, replicas)]

    got = context_move(send, 1)
    block = (tok_dev + EXTRA, 2 * head_dim)
    merged = pl.pallas_call(
        merge_kernel,
        out_shape=[struct(block, F32)] + [struct(block)] * (shards // 2 - 1),
        in_specs=[VMEM] * 2,
        out_specs=[VMEM] * (shards // 2),
        cost_estimate=cost(2),
        name="merge_cores",
    )(keep, got)
    others = [context_move(merged[step // 2], step) for step in range(2, shards, 2)]
    grad_rows, grad_kv = pl.pallas_call(
        finish_kernel,
        out_shape=[struct((tok_dev, qkv_width)), struct(block)],
        in_specs=[VMEM] * (3 + len(others)),
        out_specs=[VMEM] * 2,
        cost_estimate=cost(2),
        name="finish_rows",
    )(rope, grad_q, merged[0], *others)
    gkv = [grad_kv] + [dp_move(grad_kv, step) for step in range(1, replicas)]

    second = lax.optimization_barrier((x_halves[1][1:], gq[1:]))
    x_halves[1][1:] = [dp_move(x, step) for step, x in enumerate(second[0], 1)]

    def reduce_context(xs, gs, cols):
        rows = xs[0].shape[1] // shards
        half_rows = shards // 2 * rows
        specs = [VMEM] * (2 * replicas)
        away = pl.pallas_call(
            functools.partial(partial_kernel, replicas, 0, rows, False),
            out_shape=[struct((half_rows, cols))],
            in_specs=specs,
            out_specs=[VMEM],
            compiler_params=params(40),
            cost_estimate=cost(2 * cols / width),
            name="weights_other_core",
        )(*xs, *gs)[0]
        arrived = context_move(away, 1)
        blocks = pl.pallas_call(
            functools.partial(partial_kernel, replicas, half_rows, rows, True),
            out_shape=[struct((rows, cols), F32)] + [struct((rows, cols))] * (shards // 2 - 1),
            in_specs=specs + [VMEM],
            out_specs=[VMEM] * (shards // 2),
            compiler_params=params(40),
            cost_estimate=cost(2 * cols / width),
            name="weights_own_core",
        )(*xs, *gs, arrived)
        return [blocks[0]] + [context_move(blocks[step // 2], step) for step in range(2, shards, 2)]

    sums = [reduce_context(x_halves[half], gq, width) for half in range(2)]
    sums += [reduce_context(x_halves[half], gkv, 2 * head_dim) for half in range(2)]
    places = []
    for cols in (slice(0, width), slice(width, qkv_width)):
        for half in range(2):
            places.append((slice(half * tile, (half + 1) * tile), cols))
    grad_weight, amax = pl.pallas_call(
        functools.partial(total_kernel, [len(part) for part in sums], places),
        out_shape=[struct((slice_rows, qkv_width), F32), struct((1, 1, 2), F32)],
        in_specs=[VMEM] * (len(sums) * len(sums[0]) + replicas),
        out_specs=[VMEM] * 2,
        compiler_params=params(40),
        name="total_weights",
    )(*[x for part in sums for x in part], *gkv)
    return (grad_rows[None], grad_weight, amax)


def solution(mesh):
    in_specs = (
        P("dp", "context", None),
        P("dp", "context", None),
        P("dp", "context", None),
        P("dp", "context", None),
        P("dp", "context", None),
        P("dp", None),
        P(),
    )
    out_specs = (P("dp", "context", None), P(("dp", "context"), None), P("dp", "context", None))
    return jax.shard_map(local, mesh=mesh, in_specs=in_specs, out_specs=out_specs, check_vma=False)
```

```python
import functools
import math

import jax
import jax.numpy as jnp
import numpy as np
from jax import lax
from jax.experimental import pallas as pl
from jax.experimental.pallas import tpu as pltpu
from jax.sharding import PartitionSpec as P

THETA_BASE = 500000.0
NEG_LARGE = -1e30
DOC_VALUES = 8
EXTRA = 16
F32 = jnp.float32
BF16 = jnp.bfloat16
VMEM = pl.BlockSpec(memory_space=pltpu.VMEM)
SMEM = pl.BlockSpec(memory_space=pltpu.SMEM)
ANY = pl.BlockSpec(memory_space=pl.ANY)


def rope_tables(seq_len, head_dim):
    inverse_freq = THETA_BASE ** (-2.0 * np.arange(head_dim // 2) / head_dim)
    angles = np.arange(seq_len)[:, None] * inverse_freq[None, :]
    angles = np.concatenate([angles, angles], axis=1)
    sign = np.where(np.arange(head_dim) < head_dim // 2, 1.0, -1.0)
    return np.concatenate(
        [np.cos(angles).astype(np.float32), (np.sin(angles) * sign).astype(np.float32)], axis=1
    )


def unrotate(rows, cosine, signed_sine):
    return rows * cosine + pltpu.roll(rows, rows.shape[-1] // 2, 1) * signed_sine


def span_of(pair, half, shards):
    return pair if half == 0 else 2 * shards - 1 - pair


def spread_max(out_max, ds_max, width):
    high = ds_max.astype(BF16).astype(F32)
    middle = (ds_max - high).astype(BF16).astype(F32)
    low = ds_max - high - middle
    row = lax.broadcasted_iota(jnp.int32, (EXTRA, width), 0)
    return jnp.where(
        row == 0,
        out_max,
        jnp.where(row == 1, high, jnp.where(row == 2, middle, jnp.where(row == 3, low, 0.0))),
    )


def read_max(rows):
    wide = rows.astype(F32)
    return wide[0:1], wide[1:2] + wide[2:3] + wide[3:4]


def join_max(parts):
    pairs = [read_max(part) for part in parts]
    out_max, ds_max = pairs[0]
    for other_out, other_ds in pairs[1:]:
        out_max, ds_max = jnp.maximum(out_max, other_out), jnp.maximum(ds_max, other_ds)
    return spread_max(out_max, ds_max, parts[0].shape[1])


def attend_kernel(shards, heads, order, rope, bounds, out_top, q_cats, g_cats, *refs):
    pieces = refs[:shards]
    (gq_ref, keep_ref, send_ref, keys, values, score_buf, dprob_buf, dq_acc, dk_acc, dv_acc) = refs[shards:]
    lanes, head_dim = q_cats.shape[1:]
    span_len = lanes // heads
    tok_dev = 2 * span_len
    scale = 1.0 / math.sqrt(head_dim)
    for index in range(shards):
        rows = pl.ds(index * tok_dev, tok_dev)
        keys[rows] = pieces[index][:, :head_dim]
        values[rows] = pieces[index][:, head_dim:]
    dk_acc[...] = jnp.zeros_like(dk_acc)
    dv_acc[...] = jnp.zeros_like(dv_acc)
    ds_top = jnp.zeros((1, lanes), F32)
    sub = lax.broadcasted_iota(jnp.int32, (span_len, 1), 0)

    for half in range(2):
        count = order[half, 2, 0]
        doc_first = bounds[half, 0:1]
        query_pos = bounds[half, 1:2]
        own = pl.ds(half * span_len, span_len)
        q_cat, g_cat = q_cats.at[half], g_cats.at[half]

        def score_step(index, top):
            block = order[half, 0, index]
            key_pos = order[half, 1, index] * span_len + sub
            rows = pl.ds(pl.multiple_of(block * span_len, span_len), span_len)
            scores = lax.dot_general(
                keys[rows], q_cat[...], (((1,), (1,)), ((), ())), preferred_element_type=F32
            )
            allowed = (key_pos <= query_pos) & (key_pos >= doc_first)
            scores = jnp.where(allowed, scores, NEG_LARGE)
            score_buf[index] = scores
            dprob_buf[index] = lax.dot_general(
                values[rows], g_cat[...], (((1,), (1,)), ((), ())), preferred_element_type=F32
            )
            return jnp.maximum(top, jnp.max(scores, axis=0, keepdims=True))

        top = lax.fori_loop(0, count, score_step, jnp.full((1, lanes), NEG_LARGE, F32))

        def exp_step(index, sums):
            total, weighted = sums
            expd = jnp.exp((score_buf[index] - top) * scale)
            score_buf[index] = expd
            return (
                total + jnp.sum(expd, axis=0, keepdims=True),
                weighted + jnp.sum(expd * dprob_buf[index], axis=0, keepdims=True),
            )

        zero_row = jnp.zeros((1, lanes), F32)
        total, weighted = lax.fori_loop(0, count, exp_step, (zero_row, zero_row))
        inverse = 1.0 / total
        delta = weighted * inverse
        dq_acc[...] = jnp.zeros_like(dq_acc)

        def grad_step(index, ds_now):
            block = order[half, 0, index]
            rows = pl.ds(pl.multiple_of(block * span_len, span_len), span_len)
            probs = score_buf[index] * inverse
            dscores = probs * (dprob_buf[index] - delta)
            probs_low = probs.astype(BF16)
            ds_low = dscores.astype(BF16)
            dv_acc[rows] += jnp.dot(probs_low, g_cat[...], preferred_element_type=F32)
            dk_acc[rows] += jnp.dot(ds_low, q_cat[...], preferred_element_type=F32)
            dq_acc[...] += lax.dot_general(
                keys[rows], ds_low, (((0,), (0,)), ((), ())), preferred_element_type=F32
            )
            return jnp.maximum(ds_now, jnp.max(jnp.abs(dscores), axis=0, keepdims=True))

        ds_top = lax.fori_loop(0, count, grad_step, ds_top)
        cosine = rope[half, :, :head_dim]
        signed_sine = rope[half, :, head_dim:]
        grad_q = dq_acc[...].T * scale
        for head in range(heads):
            part = grad_q[head * span_len : (head + 1) * span_len]
            gq_ref[own, pl.ds(head * head_dim, head_dim)] = unrotate(part, cosine, signed_sine).astype(BF16)

    extra = spread_max(jnp.max(out_top[...]), jnp.max(ds_top), 2 * head_dim)
    for index in range(shards):
        rows = pl.ds(index * tok_dev, tok_dev)
        target = (keep_ref, send_ref)[index % 2]
        kind = target.dtype
        target[index // 2, :tok_dev, :head_dim] = dk_acc[rows].astype(kind)
        target[index // 2, :tok_dev, head_dim:] = dv_acc[rows].astype(kind)
        target[index // 2, tok_dev:] = extra.astype(kind)


def merge_kernel(keep_ref, got_ref, next_ref, send_ref):
    tok_dev = keep_ref.shape[1] - EXTRA
    extra = join_max([keep_ref[0, tok_dev:], got_ref[0, tok_dev:]])
    for index in range(keep_ref.shape[0]):
        both = keep_ref[index, :tok_dev] + got_ref[index, :tok_dev].astype(F32)
        target = (next_ref, send_ref)[index % 2]
        target[index // 2, :tok_dev] = both.astype(target.dtype)
        target[index // 2, tok_dev:] = extra.astype(target.dtype)


def finish_kernel(rope, gq_ref, keep_ref, got_ref, rows_ref, gkv_ref):
    tok_dev = gq_ref.shape[0]
    head_dim = keep_ref.shape[2] // 2
    total = keep_ref[0, :tok_dev] + got_ref[0, :tok_dev].astype(F32)
    extra = join_max([keep_ref[0, tok_dev:], got_ref[0, tok_dev:]])
    wide = rope[...].reshape(tok_dev, 2 * head_dim)
    grad_k = unrotate(
        total[:, :head_dim] * (1.0 / math.sqrt(head_dim)), wide[:, :head_dim], wide[:, head_dim:]
    ).astype(BF16)
    grad_v = total[:, head_dim:].astype(BF16)
    gkv_ref[:tok_dev, :head_dim] = grad_k
    gkv_ref[:tok_dev, head_dim:] = grad_v
    gkv_ref[tok_dev:] = extra.astype(BF16)
    width = gq_ref.shape[1]
    rows_ref[:, :width] = gq_ref[...]
    rows_ref[:, width : width + head_dim] = grad_k
    rows_ref[:, width + head_dim :] = grad_v


def partial_kernel(groups, count, first, adds, *refs):
    xs, gs = refs[: groups * count], refs[groups * count : (groups + 1) * count]
    rest = refs[(groups + 1) * count :]
    tok_dev = xs[0].shape[0]
    tile = xs[0].shape[1] // (2 * first[1])
    for index in range(first[1] * groups):
        block, group = index // groups, index % groups
        cols = slice((first[0] + block) * tile, (first[0] + block + 1) * tile)
        total = None
        for x_ref, g_ref in zip(xs[group * count : (group + 1) * count], gs):
            term = lax.dot_general(
                x_ref[:, cols], g_ref[:tok_dev], (((0,), (0,)), ((), ())), preferred_element_type=F32
            )
            total = term if total is None else total + term
        rows = slice(index * tile, (index + 1) * tile)
        if adds:
            total = total + rest[0][rows].astype(F32)
            target = rest[1 + block % 2]
            place = block // 2 * groups + group
            target[place * tile : (place + 1) * tile] = total.astype(target.dtype)
        else:
            rest[0][rows] = total.astype(BF16)


def total_kernel(places, *refs):
    out_ref, amax_ref = refs[-2:]
    used = 0
    for (rows, cols), count in places:
        total = refs[used][: rows.stop - rows.start]
        for ref in refs[used + 1 : used + count]:
            total = total + ref[: rows.stop - rows.start].astype(F32)
        out_ref[rows, cols] = total
        used += count
    maxima = [ref[ref.shape[0] - EXTRA :] for ref in refs[used:-2]]
    out_max, ds_max = read_max(join_max(maxima))
    lane = lax.broadcasted_iota(jnp.int32, (1, 2), 1)
    amax_ref[0] = jnp.where(lane == 0, out_max[:, :2], ds_max[:, :2])


def prepare_kernel(replicas, shards, order, tile, pair_ref, docs_ref, table_ref, q_ref, g_ref, *refs):
    rope_sems, sems, q_buf, g_buf = refs[-4:]
    packs = len(refs) > 10
    outs, (list_ref, bounds_ref, top_ref, rope_ref, q_cat, g_cat) = refs[packs : -10 - packs], refs[-10 - packs : -4 - packs]
    waits = [pltpu.make_async_copy(q_ref, q_buf, sems.at[0]), pltpu.make_async_copy(g_ref, g_buf, sems.at[1])]
    if packs:
        x_ref = refs[-5]
        waits.append(pltpu.make_async_copy(refs[0], x_ref, sems.at[2]))
    for copy in waits:
        copy.start()
    tok_dev = q_ref.shape[0]
    span_len = tok_dev // 2
    lanes, head_dim = q_cat.shape[1:]
    rep, me = lax.axis_index("dp"), lax.axis_index("context")
    pair = pair_ref[me]
    copies = []
    for half in range(2):
        start = pl.multiple_of(span_of(pair, half, shards) * span_len, 8)
        copy = pltpu.make_async_copy(table_ref.at[pl.ds(start, span_len)], rope_ref.at[half], rope_sems.at[half])
        copy.start()
        copies.append(copy)
    docs = docs_ref[...]
    starts = [jnp.sum(jnp.where(docs < value, 1.0, 0.0)) for value in range(1, DOC_VALUES)]
    lane_row = lax.broadcasted_iota(jnp.int32, (1, lanes), 1) % span_len
    for half in range(2):
        span = span_of(pair, half, shards)
        base = span * span_len
        base_f = base.astype(F32)
        first_start = jnp.float32(0.0)
        for start in starts:
            first_start = jnp.maximum(first_start, jnp.where(start <= base_f, start, 0.0))
        first_key = first_start.astype(jnp.int32)

        def listing(block, count):
            other = pair_ref[me ^ (block // 2)]
            key_span = jnp.where(block % 2 == 0, other, 2 * shards - 1 - other)
            list_ref[half, 0, count] = block
            list_ref[half, 1, count] = key_span
            needed = (key_span <= span) & (key_span * span_len + span_len > first_key)
            return count + needed.astype(jnp.int32)

        list_ref[half, 2, 0] = lax.fori_loop(0, 2 * shards, listing, jnp.int32(0))
        query_pos = base + lane_row
        query_f = query_pos.astype(F32)
        doc_start = jnp.zeros((1, lanes), F32)
        for start in starts:
            doc_start = jnp.maximum(doc_start, jnp.where(start <= query_f, start, 0.0))
        bounds_ref[half, 0:1] = doc_start.astype(jnp.int32)
        bounds_ref[half, 1:2] = query_pos
    waits[0].wait()
    waits[1].wait()
    for half in range(2):
        own = slice(half * span_len, (half + 1) * span_len)
        for head in range(q_ref.shape[1] // head_dim):
            rows = slice(head * span_len, (head + 1) * span_len)
            cols = slice(head * head_dim, (head + 1) * head_dim)
            q_cat[half, rows] = q_buf[own, cols]
            g_cat[half, rows] = g_buf[own, cols]
    top_ref[...] = jnp.max(jnp.abs(g_cat[...].astype(F32)).reshape(-1, 8, head_dim), axis=0)
    if packs:
        waits[2].wait()
        for half in range(2):
            for step in range(replicas):
                for place, relative in enumerate(order):
                    source = (((rep ^ step) * shards + (me ^ relative)) * 2 + half) * tile
                    outs[half * replicas + step][:, place * tile : (place + 1) * tile] = x_ref[
                        :, pl.ds(pl.multiple_of(source, tile), tile)
                    ]
    for copy in copies:
        copy.wait()


def params(mebibytes):
    return pltpu.CompilerParams(vmem_limit_bytes=mebibytes << 20)


def cost(microseconds):
    return pl.CostEstimate(flops=int(microseconds * 1.0e6), bytes_accessed=0, transcendentals=0)


def local(query_rows, key_rows, value_rows, out_grads, layer_input, doc_ids, pair_span):
    shards = lax.axis_size("context")
    replicas = lax.axis_size("dp")
    tok_dev = query_rows.shape[1]
    head_dim = key_rows.shape[2]
    width = query_rows.shape[2]
    heads = width // head_dim
    model_width = layer_input.shape[2]
    span_len = tok_dev // 2
    seq_len = tok_dev * shards
    qkv_width = width + 2 * head_dim
    lanes = heads * span_len
    slice_rows = model_width // (replicas * shards)
    tile = slice_rows // 2
    table = jnp.asarray(rope_tables(seq_len, head_dim))
    order = list(range(1, shards, 2)) + list(range(0, shards, 2))

    def context_move(x, step):
        return lax.ppermute(x, "context", [(i, i ^ step) for i in range(shards)])

    def dp_move(x, step):
        return lax.ppermute(x, "dp", [(i, i ^ step) for i in range(replicas)])

    def struct(shape, kind=BF16):
        return jax.ShapeDtypeStruct(shape, kind)

    own_kv = jnp.concatenate([key_rows[0], value_rows[0]], axis=1)
    pieces = [None] * shards
    pieces[0] = own_kv
    for step in range(2, shards, 2):
        pieces[step] = context_move(own_kv, step)
    pieces[1] = context_move(own_kv, 1)

    x_local = layer_input[0]
    packs = tile % 128 == 0
    outs = [struct((tok_dev, shards * tile))] * (2 * replicas if packs else 0) + [
        struct((2, 3, 2 * shards + 1), jnp.int32),
        struct((2, 2, lanes), jnp.int32),
        struct((8, head_dim), F32),
        struct((2, span_len, 2 * head_dim), F32),
        struct((2, lanes, head_dim)),
        struct((2, lanes, head_dim)),
    ]
    prepared = pl.pallas_call(
        functools.partial(prepare_kernel, replicas, shards, order, tile),
        out_shape=outs,
        in_specs=[SMEM, VMEM] + [ANY] * (3 + packs),
        out_specs=[SMEM if out.dtype == jnp.int32 and out.shape[1] == 3 else VMEM for out in outs],
        scratch_shapes=([pltpu.VMEM((tok_dev, model_width), BF16)] if packs else [])
        + [
            pltpu.SemaphoreType.DMA((2,)),
            pltpu.SemaphoreType.DMA((3,)),
            pltpu.VMEM((tok_dev, width), BF16),
            pltpu.VMEM((tok_dev, width), BF16),
        ],
        compiler_params=params(60),
        cost_estimate=cost(4),
        name="prepare",
    )(pair_span, doc_ids, table, query_rows[0], out_grads[0], *([x_local] if packs else []))
    packed = prepared[:-6]
    rope = prepared[-3]
    pieces = lax.optimization_barrier((pieces, rope))[0]
    for step in range(2, shards, 2):
        pieces[step + 1] = context_move(pieces[step], 1)
    if tile % 128:
        me, rep = lax.axis_index("context"), lax.axis_index("dp")
        parts = []
        for step in range(replicas):
            part = lax.dynamic_slice_in_dim(x_local, (rep ^ step) * shards * slice_rows, shards * slice_rows, 1)
            part = part.reshape(tok_dev, shards, 2, tile)
            parts.append(jnp.take(part, jnp.asarray(order, jnp.int32) ^ me, axis=1))
        packed = [part[:, :, half].reshape(tok_dev, shards * tile) for half in range(2) for part in parts]
    x_halves = [list(packed[:replicas]), list(packed[replicas:])]
    x_halves[0] = lax.optimization_barrier((x_halves[0], pieces[1:3]))[0]
    x_halves[0][1:] = [dp_move(x_halves[0][step], step) for step in range(1, replicas)]

    buf = (2 * shards, span_len, lanes)
    grad_q, keep, send = pl.pallas_call(
        functools.partial(attend_kernel, shards, heads),
        out_shape=[
            struct((tok_dev, width)),
            struct((shards // 2, tok_dev + EXTRA, 2 * head_dim), F32),
            struct((shards // 2, tok_dev + EXTRA, 2 * head_dim)),
        ],
        in_specs=[SMEM] + [VMEM] * (5 + shards),
        out_specs=[VMEM] * 3,
        scratch_shapes=[
            pltpu.VMEM((seq_len, head_dim), BF16),
            pltpu.VMEM((seq_len, head_dim), BF16),
            pltpu.VMEM(buf, F32),
            pltpu.VMEM(buf, F32),
            pltpu.VMEM((head_dim, lanes), F32),
            pltpu.VMEM((seq_len, head_dim), F32),
            pltpu.VMEM((seq_len, head_dim), F32),
        ],
        compiler_params=params(60),
        cost_estimate=cost(12),
        name="attend",
    )(prepared[-6], rope, prepared[-5], prepared[-4], prepared[-2], prepared[-1], *pieces)

    grad_q, x_halves[0] = lax.optimization_barrier((grad_q, x_halves[0]))
    gq = [grad_q] + [dp_move(grad_q, step) for step in range(1, replicas)]

    block = (tok_dev + EXTRA, 2 * head_dim)
    got, step = context_move(send, 1), 2
    while step < shards:
        count = shards // 2 // step
        keep, send = pl.pallas_call(
            merge_kernel,
            out_shape=[struct((count,) + block, F32), struct((count,) + block)],
            in_specs=[VMEM] * 2,
            out_specs=[VMEM] * 2,
            cost_estimate=cost(2),
            name="merge_rows",
        )(keep, got)
        got, step = context_move(send, step), step * 2

    half_shards = shards // 2

    def other_core(groups, gs):
        rows, cols = len(groups) * tile, gs[0].shape[1]
        return pl.pallas_call(
            functools.partial(partial_kernel, len(groups), replicas, (0, half_shards), False),
            out_shape=struct((half_shards * rows, cols)),
            in_specs=[VMEM] * ((len(groups) + 1) * replicas),
            out_specs=VMEM,
            compiler_params=params(16),
            cost_estimate=cost(2),
            name="weights_other_core",
        )(*[x for xs in groups for x in xs], *gs)

    def own_core(groups, gs, arrived):
        rows, cols = len(groups) * tile, gs[0].shape[1]
        return pl.pallas_call(
            functools.partial(partial_kernel, len(groups), replicas, (half_shards, half_shards), True),
            out_shape=[struct((half_shards // 2 * rows, cols), F32), struct((half_shards // 2 * rows, cols))],
            in_specs=[VMEM] * ((len(groups) + 1) * replicas + 1),
            out_specs=[VMEM] * 2,
            compiler_params=params(16),
            cost_estimate=cost(2),
            name="weights_own_core",
        )(*[x for xs in groups for x in xs], *gs, arrived)

    def split_blocks(x, rows):
        parts = x.reshape(-1, 2, rows, x.shape[1])
        return parts[:, 0].reshape(-1, x.shape[1]), parts[:, 1].reshape(-1, x.shape[1])

    def next_terms(kept, got, rows):
        kept_even, kept_odd = split_blocks(kept, rows)
        got_even, got_odd = split_blocks(got, rows)
        return kept_even + got_even.astype(F32), (kept_odd + got_odd.astype(F32)).astype(BF16)

    def tie(value, *others):
        return lax.optimization_barrier((value, others))[0]

    gq = tie(gq, keep, got)
    away = other_core([x_halves[0]], gq)
    arrived = context_move(away, 1)
    keep, got = tie((keep, got), away)
    grad_rows, grad_kv = pl.pallas_call(
        finish_kernel,
        out_shape=[struct((tok_dev, qkv_width)), struct(block)],
        in_specs=[VMEM] * 4,
        out_specs=[VMEM] * 2,
        cost_estimate=cost(2),
        name="finish_rows",
    )(rope, grad_q, keep, got)
    second = tie(x_halves[1][1:], gq)
    x_halves[1][1:] = [dp_move(x, step) for step, x in enumerate(second, 1)]
    gkv = [grad_kv] + [dp_move(grad_kv, step) for step in range(1, replicas)]

    def first_steps(groups, gs, arrived):
        kept, sent = own_core(groups, gs, arrived)
        return kept, context_move(sent, 2)

    def last_steps(kept, got, rows):
        terms, step, sent = [kept, got], 4, got
        while step < shards:
            kept, sent = next_terms(kept, got, rows)
            got, step = context_move(sent, step), step * 2
            terms.append(got)
        return terms, sent

    first = first_steps([x_halves[0]], gq, tie(arrived, grad_kv))
    first, sent = last_steps(*first, tile)
    x_halves[1] = tie(x_halves[1], first)
    away = other_core([x_halves[1]], gq)
    arrived = context_move(away, 1)
    second = first_steps([x_halves[1]], gq, arrived)
    gkv = tie(gkv, second[0])
    away = other_core(x_halves, gkv)
    arrived = context_move(away, 1)
    second, sent = last_steps(*second, tile)
    third = first_steps(x_halves, gkv, tie(arrived, sent))
    third, sent = last_steps(*third, 2 * tile)
    terms = [first, second, third]
    places = [
        ((slice(0, tile), slice(0, width)), len(terms[0])),
        ((slice(tile, 2 * tile), slice(0, width)), len(terms[1])),
        ((slice(0, 2 * tile), slice(width, qkv_width)), len(terms[2])),
    ]
    grad_weight, amax = pl.pallas_call(
        functools.partial(total_kernel, places),
        out_shape=[struct((slice_rows, qkv_width), F32), struct((1, 1, 2), F32)],
        in_specs=[VMEM] * (sum(len(part) for part in terms) + replicas),
        out_specs=[VMEM] * 2,
        compiler_params=params(16),
        name="total_weights",
    )(*[x for part in terms for x in part], *gkv)
    return (grad_rows[None], grad_weight, amax)


def solution(mesh):
    in_specs = (
        P("dp", "context", None),
        P("dp", "context", None),
        P("dp", "context", None),
        P("dp", "context", None),
        P("dp", "context", None),
        P("dp", None),
        P(),
    )
    out_specs = (P("dp", "context", None), P(("dp", "context"), None), P("dp", "context", None))
    return jax.shard_map(local, mesh=mesh, in_specs=in_specs, out_specs=out_specs, check_vma=False)
```

```python
import functools
import math

import jax
import jax.numpy as jnp
import numpy as np
from jax import lax
from jax.experimental import pallas as pl
from jax.experimental.pallas import tpu as pltpu
from jax.sharding import PartitionSpec as P

THETA_BASE = 500000.0
NEG_LARGE = -1e30
DOC_VALUES = 8
EXTRA = 16
F32 = jnp.float32
BF16 = jnp.bfloat16
VMEM = pl.BlockSpec(memory_space=pltpu.VMEM)
SMEM = pl.BlockSpec(memory_space=pltpu.SMEM)
ANY = pl.BlockSpec(memory_space=pl.ANY)


def rope_tables(seq_len, head_dim):
    inverse_freq = THETA_BASE ** (-2.0 * np.arange(head_dim // 2) / head_dim)
    angles = np.arange(seq_len)[:, None] * inverse_freq[None, :]
    angles = np.concatenate([angles, angles], axis=1)
    sign = np.where(np.arange(head_dim) < head_dim // 2, 1.0, -1.0)
    return np.concatenate(
        [np.cos(angles).astype(np.float32), (np.sin(angles) * sign).astype(np.float32)], axis=1
    )


def unrotate(rows, cosine, signed_sine):
    return rows * cosine + pltpu.roll(rows, rows.shape[-1] // 2, 1) * signed_sine


def span_of(pair, half, shards):
    return pair if half == 0 else 2 * shards - 1 - pair


def spread_max(out_max, ds_max, width):
    high = ds_max.astype(BF16).astype(F32)
    middle = (ds_max - high).astype(BF16).astype(F32)
    low = ds_max - high - middle
    row = lax.broadcasted_iota(jnp.int32, (EXTRA, width), 0)
    return jnp.where(
        row == 0,
        out_max,
        jnp.where(row == 1, high, jnp.where(row == 2, middle, jnp.where(row == 3, low, 0.0))),
    )


def read_max(rows):
    wide = rows.astype(F32)
    return wide[0:1], wide[1:2] + wide[2:3] + wide[3:4]


def join_max(parts):
    pairs = [read_max(part) for part in parts]
    out_max, ds_max = pairs[0]
    for other_out, other_ds in pairs[1:]:
        out_max, ds_max = jnp.maximum(out_max, other_out), jnp.maximum(ds_max, other_ds)
    return spread_max(out_max, ds_max, parts[0].shape[1])


def attend_kernel(shards, heads, order, rope, bounds, out_top, q_cats, g_cats, kv_ref, *refs):
    gq_ref, keep_ref, send_ref, key_list, value_list, score_buf, dprob_buf, dq_acc, dk_acc, dv_acc = refs
    lanes, head_dim = q_cats.shape[1:]
    span_len = lanes // heads
    tok_dev = 2 * span_len
    scale = 1.0 / math.sqrt(head_dim)
    me = lax.axis_index("context")
    dk_acc[...] = jnp.zeros_like(dk_acc)
    dv_acc[...] = jnp.zeros_like(dv_acc)
    ds_top = jnp.zeros((1, lanes), F32)
    sub = lax.broadcasted_iota(jnp.int32, (2 * span_len, 1), 0)

    for half in range(2):
        count = order[half, 2, 0]
        steps = (count + 1) // 2

        def listing(index, unused):
            source = pl.ds(pl.multiple_of(order[half, 0, index] * span_len, span_len), span_len)
            target = pl.ds(pl.multiple_of(index * span_len, span_len), span_len)
            key_list[target] = kv_ref[source, :head_dim]
            value_list[target] = kv_ref[source, head_dim:]
            return unused

        lax.fori_loop(0, count, listing, 0)
        spare = pl.ds(pl.multiple_of(count * span_len, span_len), span_len)
        key_list[spare] = jnp.zeros((span_len, head_dim), BF16)
        value_list[spare] = jnp.zeros((span_len, head_dim), BF16)
        doc_first = bounds[half, 0:1]
        query_pos = bounds[half, 1:2]
        own = pl.ds(half * span_len, span_len)
        q_cat, g_cat = q_cats.at[half], g_cats.at[half]

        def score_step(index, top):
            rows = pl.ds(pl.multiple_of(index * 2 * span_len, 2 * span_len), 2 * span_len)
            start = jnp.where(sub < span_len, order[half, 1, 2 * index], order[half, 1, 2 * index + 1] - 1)
            key_pos = start * span_len + sub
            scores = lax.dot_general(
                key_list[rows], q_cat[...], (((1,), (1,)), ((), ())), preferred_element_type=F32
            )
            allowed = (key_pos <= query_pos) & (key_pos >= doc_first)
            scores = jnp.where(allowed, scores, NEG_LARGE)
            score_buf[index] = scores
            dprob_buf[index] = lax.dot_general(
                value_list[rows], g_cat[...], (((1,), (1,)), ((), ())), preferred_element_type=F32
            )
            return jnp.maximum(top, jnp.max(scores, axis=0, keepdims=True))

        top = lax.fori_loop(0, steps, score_step, jnp.full((1, lanes), NEG_LARGE, F32))

        def exp_step(index, sums):
            total, weighted = sums
            expd = jnp.exp((score_buf[index] - top) * scale)
            score_buf[index] = expd
            return (
                total + jnp.sum(expd, axis=0, keepdims=True),
                weighted + jnp.sum(expd * dprob_buf[index], axis=0, keepdims=True),
            )

        zero_row = jnp.zeros((1, lanes), F32)
        total, weighted = lax.fori_loop(0, steps, exp_step, (zero_row, zero_row))
        inverse = 1.0 / total
        delta = weighted * inverse
        dq_acc[...] = jnp.zeros_like(dq_acc)

        def grad_step(index, ds_now):
            rows = pl.ds(pl.multiple_of(index * 2 * span_len, 2 * span_len), 2 * span_len)
            probs = score_buf[index] * inverse
            dscores = probs * (dprob_buf[index] - delta)
            probs_low = probs.astype(BF16)
            ds_low = dscores.astype(BF16)
            grad_v = jnp.dot(probs_low, g_cat[...], preferred_element_type=F32)
            grad_k = jnp.dot(ds_low, q_cat[...], preferred_element_type=F32)
            for part in range(2):
                block = pl.ds(pl.multiple_of(order[half, 0, 2 * index + part] * span_len, span_len), span_len)
                own_part = slice(part * span_len, (part + 1) * span_len)
                dv_acc[block] += grad_v[own_part]
                dk_acc[block] += grad_k[own_part]
            dq_acc[...] += lax.dot_general(
                key_list[rows], ds_low, (((0,), (0,)), ((), ())), preferred_element_type=F32
            )
            return jnp.maximum(ds_now, jnp.max(jnp.abs(dscores), axis=0, keepdims=True))

        ds_top = lax.fori_loop(0, steps, grad_step, ds_top)
        cosine = rope[half, :, :head_dim]
        signed_sine = rope[half, :, head_dim:]
        grad_q = dq_acc[...].T * scale
        for head in range(heads):
            part = grad_q[head * span_len : (head + 1) * span_len]
            gq_ref[own, pl.ds(head * head_dim, head_dim)] = unrotate(part, cosine, signed_sine).astype(BF16)

    extra = spread_max(jnp.max(out_top[...]), jnp.max(ds_top), 2 * head_dim)
    for index in range(shards):
        rows = pl.ds(pl.multiple_of((me ^ index) * tok_dev, tok_dev), tok_dev)
        target = (keep_ref, send_ref)[index % 2]
        kind = target.dtype
        target[index // 2, :tok_dev, :head_dim] = dk_acc[rows].astype(kind)
        target[index // 2, :tok_dev, head_dim:] = dv_acc[rows].astype(kind)
        target[index // 2, tok_dev:] = extra.astype(kind)


def merge_kernel(keep_ref, got_ref, next_ref, send_ref):
    tok_dev = keep_ref.shape[1] - EXTRA
    extra = join_max([keep_ref[0, tok_dev:], got_ref[0, tok_dev:]])
    for index in range(keep_ref.shape[0]):
        both = keep_ref[index, :tok_dev] + got_ref[index, :tok_dev].astype(F32)
        target = (next_ref, send_ref)[index % 2]
        target[index // 2, :tok_dev] = both.astype(target.dtype)
        target[index // 2, tok_dev:] = extra.astype(target.dtype)


def finish_kernel(rope, gq_ref, keep_ref, got_ref, rows_ref, gkv_ref):
    tok_dev, width = gq_ref.shape
    head_dim = keep_ref.shape[2] // 2
    total = keep_ref[0, :tok_dev] + got_ref[0, :tok_dev].astype(F32)
    extra = join_max([keep_ref[0, tok_dev:], got_ref[0, tok_dev:]])
    wide = rope[...].reshape(tok_dev, 2 * head_dim)
    grad_k = unrotate(
        total[:, :head_dim] * (1.0 / math.sqrt(head_dim)), wide[:, :head_dim], wide[:, head_dim:]
    ).astype(BF16)
    grad_v = total[:, head_dim:].astype(BF16)
    gkv_ref[:tok_dev, :head_dim] = grad_k
    gkv_ref[:tok_dev, head_dim:] = grad_v
    gkv_ref[tok_dev:] = extra.astype(BF16)
    rows_ref[:, :width] = gq_ref[...]
    rows_ref[:, width : width + head_dim] = grad_k
    rows_ref[:, width + head_dim :] = grad_v


def partial_kernel(count, firsts, blocks, tile, adds, *refs):
    groups = len(firsts)
    xs, gs = refs[: groups * count], refs[groups * count : (groups + 1) * count]
    rest = refs[(groups + 1) * count :]
    tok_dev = xs[0].shape[0]
    for index in range(blocks * groups):
        block, group = index // groups, index % groups
        cols = slice((firsts[group] + block) * tile, (firsts[group] + block + 1) * tile)
        total = None
        for x_ref, g_ref in zip(xs[group * count : (group + 1) * count], gs):
            term = lax.dot_general(
                x_ref[:, cols], g_ref[:tok_dev], (((0,), (0,)), ((), ())), preferred_element_type=F32
            )
            total = term if total is None else total + term
        rows = slice(index * tile, (index + 1) * tile)
        if adds:
            total = total + rest[0][rows].astype(F32)
            target = rest[1 + block % 2]
            place = block // 2 * groups + group
            target[place * tile : (place + 1) * tile] = total.astype(target.dtype)
        else:
            rest[0][rows] = total.astype(BF16)


def total_kernel(places, *refs):
    out_ref, amax_ref = refs[-2:]
    used = 0
    for (rows, cols), count in places:
        total = refs[used][: rows.stop - rows.start]
        for ref in refs[used + 1 : used + count]:
            total = total + ref[: rows.stop - rows.start].astype(F32)
        out_ref[rows, cols] = total
        used += count
    maxima = [ref[ref.shape[0] - EXTRA :] for ref in refs[used:-2]]
    out_max, ds_max = read_max(join_max(maxima))
    lane = lax.broadcasted_iota(jnp.int32, (1, 2), 1)
    amax_ref[0] = jnp.where(lane == 0, out_max[:, :2], ds_max[:, :2])


def prepare_kernel(replicas, shards, order, pair_ref, docs_ref, k_ref, v_ref, table_ref, q_ref, g_ref, *refs):
    rope_sems, sems, x_sems, q_buf, g_buf = refs[-5:]
    x_refs, outs = refs[:-12], refs[-12:-5]
    list_ref, kv_ref, bounds_ref, top_ref, rope_ref, q_cat, g_cat = outs
    x_copies = []
    if x_refs:
        rep, own = lax.axis_index("dp"), lax.axis_index("context")
        tile = x_refs[1].shape[1] // shards
        for step in range(replicas):
            for place, relative in enumerate(order):
                block = (rep ^ step) * shards + (own ^ relative)
                half = place // (shards // 2)
                spots = ((0, x_refs[1 + step], place), (1, x_refs[1 + (1 + half) * replicas + step], place % (shards // 2)))
                for part, target, spot in spots:
                    source = pl.multiple_of((block * 2 + part) * tile, tile)
                    copy = pltpu.make_async_copy(
                        x_refs[0].at[:, pl.ds(source, tile)],
                        target.at[:, pl.ds(spot * tile, tile)],
                        x_sems.at[part, step, place],
                    )
                    copy.start()
                    x_copies.append(copy)
    kv_ref[:, : k_ref.shape[1]] = k_ref[...]
    kv_ref[:, k_ref.shape[1] :] = v_ref[...]
    waits = [pltpu.make_async_copy(q_ref, q_buf, sems.at[0]), pltpu.make_async_copy(g_ref, g_buf, sems.at[1])]
    for copy in waits:
        copy.start()
    tok_dev = q_ref.shape[0]
    span_len = tok_dev // 2
    lanes, head_dim = q_cat.shape[1:]
    me = lax.axis_index("context")
    pair = pair_ref[me]
    copies = []
    for half in range(2):
        start = pl.multiple_of(span_of(pair, half, shards) * span_len, 8)
        copy = pltpu.make_async_copy(table_ref.at[pl.ds(start, span_len)], rope_ref.at[half], rope_sems.at[half])
        copy.start()
        copies.append(copy)
    docs = docs_ref[...]
    starts = [jnp.sum(jnp.where(docs < value, 1.0, 0.0)) for value in range(1, DOC_VALUES)]
    lane_row = lax.broadcasted_iota(jnp.int32, (1, lanes), 1) % span_len
    for half in range(2):
        span = span_of(pair, half, shards)
        base = span * span_len
        base_f = base.astype(F32)
        first_start = jnp.float32(0.0)
        for start in starts:
            first_start = jnp.maximum(first_start, jnp.where(start <= base_f, start, 0.0))
        first_key = first_start.astype(jnp.int32)

        def listing(block, count):
            other = pair_ref[block // 2]
            key_span = jnp.where(block % 2 == 0, other, 2 * shards - 1 - other)
            list_ref[half, 0, count] = block
            list_ref[half, 1, count] = key_span
            needed = (key_span <= span) & (key_span * span_len + span_len > first_key)
            return count + needed.astype(jnp.int32)

        count = lax.fori_loop(0, 2 * shards, listing, jnp.int32(0))
        list_ref[half, 2, 0] = count
        list_ref[half, 0, count] = 2 * shards
        list_ref[half, 1, count] = 2 * shards
        query_pos = base + lane_row
        query_f = query_pos.astype(F32)
        doc_start = jnp.zeros((1, lanes), F32)
        for start in starts:
            doc_start = jnp.maximum(doc_start, jnp.where(start <= query_f, start, 0.0))
        bounds_ref[half, 0:1] = doc_start.astype(jnp.int32)
        bounds_ref[half, 1:2] = query_pos
    waits[0].wait()
    waits[1].wait()
    for half in range(2):
        own = slice(half * span_len, (half + 1) * span_len)
        for head in range(q_ref.shape[1] // head_dim):
            rows = slice(head * span_len, (head + 1) * span_len)
            cols = slice(head * head_dim, (head + 1) * head_dim)
            q_cat[half, rows] = q_buf[own, cols]
            g_cat[half, rows] = g_buf[own, cols]
    top_ref[...] = jnp.max(jnp.abs(g_cat[...].astype(F32)).reshape(-1, 8, head_dim), axis=0)
    for copy in copies + x_copies:
        copy.wait()


def params(mebibytes):
    return pltpu.CompilerParams(vmem_limit_bytes=mebibytes << 20)


def cost(microseconds):
    return pl.CostEstimate(flops=int(microseconds * 1.0e6), bytes_accessed=0, transcendentals=0)


def local(query_rows, key_rows, value_rows, out_grads, layer_input, doc_ids, pair_span):
    shards = lax.axis_size("context")
    replicas = lax.axis_size("dp")
    tok_dev = query_rows.shape[1]
    head_dim = key_rows.shape[2]
    width = query_rows.shape[2]
    heads = width // head_dim
    model_width = layer_input.shape[2]
    span_len = tok_dev // 2
    seq_len = tok_dev * shards
    qkv_width = width + 2 * head_dim
    lanes = heads * span_len
    slice_rows = model_width // (replicas * shards)
    tile = slice_rows // 2
    packs = tile % 128 == 0
    half_shards = shards // 2
    table = jnp.asarray(rope_tables(seq_len, head_dim))
    order = list(range(1, shards, 2)) + list(range(0, shards, 2))

    def context_move(x, step):
        return lax.ppermute(x, "context", [(i, i ^ step) for i in range(shards)])

    def dp_move(x, step):
        return lax.ppermute(x, "dp", [(i, i ^ step) for i in range(replicas)])

    def struct(shape, kind=BF16):
        return jax.ShapeDtypeStruct(shape, kind)

    outs = [
        struct((2, 3, 2 * shards + 1), jnp.int32),
        struct((tok_dev, 2 * head_dim)),
        struct((2, 2, lanes), jnp.int32),
        struct((8, head_dim), F32),
        struct((2, span_len, 2 * head_dim), F32),
        struct((2, lanes, head_dim)),
        struct((2, lanes, head_dim)),
    ]
    x_shapes = [(tok_dev, count * tile) for count in (shards, half_shards, half_shards) for _ in range(replicas)]
    if packs:
        outs = [struct(shape) for shape in x_shapes] + outs
    prepared = pl.pallas_call(
        functools.partial(prepare_kernel, replicas, shards, order),
        out_shape=outs,
        in_specs=[SMEM] + [VMEM] * 3 + [ANY] * (3 + packs),
        out_specs=[VMEM] * (len(outs) - 7) + [SMEM] + [VMEM] * 6,
        scratch_shapes=[
            pltpu.SemaphoreType.DMA((2,)),
            pltpu.SemaphoreType.DMA((2,)),
            pltpu.SemaphoreType.DMA((2, replicas, shards)),
            pltpu.VMEM((tok_dev, width), BF16),
            pltpu.VMEM((tok_dev, width), BF16),
        ],
        compiler_params=params(60),
        cost_estimate=cost(4),
        name="prepare",
    )(pair_span, doc_ids, key_rows[0], value_rows[0], table, query_rows[0], out_grads[0], *([layer_input[0]] if packs else []))
    order_list, own_kv, bounds, out_top, rope, q_cats, g_cats = prepared[-7:]
    if packs:
        columns = [list(prepared[first : first + replicas]) for first in range(0, 3 * replicas, replicas)]
    else:
        me, rep = lax.axis_index("context"), lax.axis_index("dp")
        columns = [[], [], []]
        for step in range(replicas):
            part = lax.dynamic_slice_in_dim(layer_input[0], (rep ^ step) * shards * slice_rows, shards * slice_rows, 1)
            part = jnp.take(part.reshape(tok_dev, shards, 2, tile), jnp.asarray(order, jnp.int32) ^ me, axis=1)
            pieces = part[:, :, 0], part[:, :half_shards, 1], part[:, half_shards:, 1]
            for group, piece in zip(columns, pieces):
                group.append(piece.reshape(tok_dev, -1))
    x_first, x_odd, x_even = columns

    def tie(value, *others):
        return lax.optimization_barrier((value, others))[0]

    def exchange(parts):
        return [parts[0]] + [dp_move(parts[step], step) for step in range(1, replicas)]

    x_first = exchange(x_first)
    kv_all = lax.all_gather(own_kv, "context", axis=0, tiled=True)
    x_odd = exchange(tie(x_odd, kv_all, x_first))

    buf = (shards + 1, 2 * span_len, lanes)
    padded = (seq_len + 2 * span_len, head_dim)
    grad_q, keep, send = pl.pallas_call(
        functools.partial(attend_kernel, shards, heads),
        out_shape=[
            struct((tok_dev, width)),
            struct((shards // 2, tok_dev + EXTRA, 2 * head_dim), F32),
            struct((shards // 2, tok_dev + EXTRA, 2 * head_dim)),
        ],
        in_specs=[SMEM] + [VMEM] * 6,
        out_specs=[VMEM] * 3,
        scratch_shapes=[
            pltpu.VMEM(padded, BF16),
            pltpu.VMEM(padded, BF16),
            pltpu.VMEM(buf, F32),
            pltpu.VMEM(buf, F32),
            pltpu.VMEM((head_dim, lanes), F32),
            pltpu.VMEM(padded, F32),
            pltpu.VMEM(padded, F32),
        ],
        compiler_params=params(60),
        cost_estimate=cost(12),
        name="attend",
    )(order_list, rope, bounds, out_top, q_cats, g_cats, kv_all)

    grad_q, send = tie((grad_q, send), x_odd)
    gq = exchange([grad_q] * replicas)

    block = (tok_dev + EXTRA, 2 * head_dim)
    got, step = context_move(send, 1), 2
    while step < shards:
        count = shards // 2 // step
        keep, send = pl.pallas_call(
            merge_kernel,
            out_shape=[struct((count,) + block, F32), struct((count,) + block)],
            in_specs=[VMEM] * 2,
            out_specs=[VMEM] * 2,
            cost_estimate=cost(2),
            name="merge_rows",
        )(keep, got)
        got, step = context_move(send, step), step * 2

    def partial_weights(groups, gs, arrived=None):
        firsts, parts = [first for first, _ in groups], [x for _, xs in groups for x in xs]
        rows, cols = half_shards * len(groups) * tile, gs[0].shape[1]
        adds = arrived is not None
        out_shape = [struct((rows, cols))]
        if adds:
            out_shape = [struct((rows // 2, cols), F32), struct((rows // 2, cols))]
        result = pl.pallas_call(
            functools.partial(partial_kernel, replicas, firsts, half_shards, tile, adds),
            out_shape=out_shape,
            in_specs=[VMEM] * (len(parts) + replicas + adds),
            out_specs=[VMEM] * len(out_shape),
            compiler_params=params(16),
            cost_estimate=cost(2),
            name="weights_own_core" if adds else "weights_other_core",
        )(*parts, *gs, *([arrived] if adds else []))
        return result if adds else result[0]

    def split_blocks(x, rows):
        parts = x.reshape(-1, 2, rows, x.shape[1])
        return parts[:, 0].reshape(-1, x.shape[1]), parts[:, 1].reshape(-1, x.shape[1])

    def next_terms(kept, got, rows):
        kept_even, kept_odd = split_blocks(kept, rows)
        got_even, got_odd = split_blocks(got, rows)
        return kept_even + got_even.astype(F32), (kept_odd + got_odd.astype(F32)).astype(BF16)

    def last_steps(kept, got, rows):
        terms, step, sent = [kept, got], 4, got
        while step < shards:
            kept, sent = next_terms(kept, got, rows)
            got, step = context_move(sent, step), step * 2
            terms.append(got)
        return terms, sent

    gq = tie(gq, keep, got)
    away = partial_weights([(0, x_first)], gq)
    arrived = context_move(away, 1)
    keep, got = tie((keep, got), away)
    grad_rows, grad_kv = pl.pallas_call(
        finish_kernel,
        out_shape=[struct((tok_dev, qkv_width)), struct(block)],
        in_specs=[VMEM] * 4,
        out_specs=[VMEM] * 2,
        cost_estimate=cost(2),
        name="finish_rows",
    )(rope, grad_q, keep, got)
    x_even = exchange(tie(x_even, gq))
    gkv = exchange([grad_kv] * replicas)
    kept, sent = partial_weights([(half_shards, x_first)], gq, tie(arrived, grad_kv))
    first = kept, context_move(sent, 2)
    away = partial_weights([(0, tie(x_odd, sent))], gq)
    arrived = context_move(away, 1)
    first, sent = last_steps(*first, tile)
    kept, sent = partial_weights([(0, x_even)], gq, tie(arrived, sent))
    second = kept, context_move(sent, 2)
    away = partial_weights([(0, x_first), (0, x_odd)], tie(gkv, sent, first))
    arrived = context_move(away, 1)
    second, sent = last_steps(*second, tile)
    kept, sent = partial_weights([(half_shards, x_first), (0, x_even)], gkv, tie(arrived, sent))
    third = last_steps(kept, context_move(sent, 2), 2 * tile)[0]
    terms = [first, second, third]
    upper, lower, full = slice(0, tile), slice(tile, 2 * tile), slice(0, width)
    spots = [(upper, full), (lower, full), (slice(0, 2 * tile), slice(width, qkv_width))]
    places = [(spot, len(part)) for spot, part in zip(spots, terms)]
    grad_weight, amax = pl.pallas_call(
        functools.partial(total_kernel, places),
        out_shape=[struct((slice_rows, qkv_width), F32), struct((1, 1, 2), F32)],
        in_specs=[VMEM] * (sum(len(part) for part in terms) + replicas),
        out_specs=[VMEM] * 2,
        compiler_params=params(16),
        name="total_weights",
    )(*[x for part in terms for x in part], *gkv)
    return (grad_rows[None], grad_weight, amax)


def solution(mesh):
    in_specs = (
        P("dp", "context", None),
        P("dp", "context", None),
        P("dp", "context", None),
        P("dp", "context", None),
        P("dp", "context", None),
        P("dp", None),
        P(),
    )
    out_specs = (P("dp", "context", None), P(("dp", "context"), None), P("dp", "context", None))
    return jax.shard_map(local, mesh=mesh, in_specs=in_specs, out_specs=out_specs, check_vma=False)
```

```python
import functools
import math

import jax
import jax.numpy as jnp
import numpy as np
from jax import lax
from jax.experimental import pallas as pl
from jax.experimental.pallas import tpu as pltpu
from jax.sharding import PartitionSpec as P

THETA_BASE = 500000.0
NEG_LARGE = -1e30
DOC_VALUES = 8
EXTRA = 16
F32 = jnp.float32
BF16 = jnp.bfloat16
VMEM = pl.BlockSpec(memory_space=pltpu.VMEM)
SMEM = pl.BlockSpec(memory_space=pltpu.SMEM)
ANY = pl.BlockSpec(memory_space=pl.ANY)


def rope_tables(seq_len, head_dim):
    inverse_freq = THETA_BASE ** (-2.0 * np.arange(head_dim // 2) / head_dim)
    angles = np.arange(seq_len)[:, None] * inverse_freq[None, :]
    angles = np.concatenate([angles, angles], axis=1)
    sign = np.where(np.arange(head_dim) < head_dim // 2, 1.0, -1.0)
    return np.concatenate(
        [np.cos(angles).astype(np.float32), (np.sin(angles) * sign).astype(np.float32)], axis=1
    )


def unrotate(rows, cosine, signed_sine):
    return rows * cosine + pltpu.roll(rows, rows.shape[-1] // 2, 1) * signed_sine


def span_of(pair, half, shards):
    return pair if half == 0 else 2 * shards - 1 - pair


def spread_max(out_max, ds_max, width):
    high = ds_max.astype(BF16).astype(F32)
    middle = (ds_max - high).astype(BF16).astype(F32)
    low = ds_max - high - middle
    row = lax.broadcasted_iota(jnp.int32, (EXTRA, width), 0)
    return jnp.where(
        row == 0,
        out_max,
        jnp.where(row == 1, high, jnp.where(row == 2, middle, jnp.where(row == 3, low, 0.0))),
    )


def read_max(rows):
    wide = rows.astype(F32)
    return wide[0:1], wide[1:2] + wide[2:3] + wide[3:4]


def join_max(parts):
    pairs = [read_max(part) for part in parts]
    out_max, ds_max = pairs[0]
    for other_out, other_ds in pairs[1:]:
        out_max, ds_max = jnp.maximum(out_max, other_out), jnp.maximum(ds_max, other_ds)
    return spread_max(out_max, ds_max, parts[0].shape[1])


def attend_kernel(shards, heads, order, rope, bounds, out_top, q_cats, g_cats, kv_ref, *refs):
    gq_ref, keep_ref, send_ref, key_list, value_list, score_buf, dprob_buf, dq_acc, dk_acc, dv_acc = refs
    lanes, head_dim = q_cats.shape[1:]
    span_len = lanes // heads
    tok_dev = 2 * span_len
    scale = 1.0 / math.sqrt(head_dim)
    me = lax.axis_index("context")
    dk_acc[...] = jnp.zeros_like(dk_acc)
    dv_acc[...] = jnp.zeros_like(dv_acc)
    ds_top = jnp.zeros((1, lanes), F32)
    sub = lax.broadcasted_iota(jnp.int32, (2 * span_len, 1), 0)

    for half in range(2):
        count = order[half, 2, 0]
        steps = (count + 1) // 2

        def listing(index, unused):
            source = pl.ds(pl.multiple_of(order[half, 0, index] * span_len, span_len), span_len)
            target = pl.ds(pl.multiple_of(index * span_len, span_len), span_len)
            key_list[target] = kv_ref[source, :head_dim]
            value_list[target] = kv_ref[source, head_dim:]
            return unused

        lax.fori_loop(0, count, listing, 0)
        spare = pl.ds(pl.multiple_of(count * span_len, span_len), span_len)
        key_list[spare] = jnp.zeros((span_len, head_dim), BF16)
        value_list[spare] = jnp.zeros((span_len, head_dim), BF16)
        doc_first = bounds[half, 0:1]
        query_pos = bounds[half, 1:2]
        own = pl.ds(half * span_len, span_len)
        q_cat, g_cat = q_cats.at[half], g_cats.at[half]

        def score_step(index, top):
            rows = pl.ds(pl.multiple_of(index * 2 * span_len, 2 * span_len), 2 * span_len)
            start = jnp.where(sub < span_len, order[half, 1, 2 * index], order[half, 1, 2 * index + 1] - 1)
            key_pos = start * span_len + sub
            scores = lax.dot_general(
                key_list[rows], q_cat[...], (((1,), (1,)), ((), ())), preferred_element_type=F32
            )
            allowed = (key_pos <= query_pos) & (key_pos >= doc_first)
            scores = jnp.where(allowed, scores, NEG_LARGE)
            score_buf[index] = scores
            dprob_buf[index] = lax.dot_general(
                value_list[rows], g_cat[...], (((1,), (1,)), ((), ())), preferred_element_type=F32
            )
            return jnp.maximum(top, jnp.max(scores, axis=0, keepdims=True))

        top = lax.fori_loop(0, steps, score_step, jnp.full((1, lanes), NEG_LARGE, F32))

        def exp_step(index, sums):
            total, weighted = sums
            expd = jnp.exp((score_buf[index] - top) * scale)
            score_buf[index] = expd
            return (
                total + jnp.sum(expd, axis=0, keepdims=True),
                weighted + jnp.sum(expd * dprob_buf[index], axis=0, keepdims=True),
            )

        zero_row = jnp.zeros((1, lanes), F32)
        total, weighted = lax.fori_loop(0, steps, exp_step, (zero_row, zero_row))
        inverse = 1.0 / total
        delta = weighted * inverse
        dq_acc[...] = jnp.zeros_like(dq_acc)

        def grad_step(index, ds_now):
            rows = pl.ds(pl.multiple_of(index * 2 * span_len, 2 * span_len), 2 * span_len)
            probs = score_buf[index] * inverse
            dscores = probs * (dprob_buf[index] - delta)
            probs_low = probs.astype(BF16)
            ds_low = dscores.astype(BF16)
            grad_v = jnp.dot(probs_low, g_cat[...], preferred_element_type=F32)
            grad_k = jnp.dot(ds_low, q_cat[...], preferred_element_type=F32)
            for part in range(2):
                block = pl.ds(pl.multiple_of(order[half, 0, 2 * index + part] * span_len, span_len), span_len)
                own_part = slice(part * span_len, (part + 1) * span_len)
                dv_acc[block] += grad_v[own_part]
                dk_acc[block] += grad_k[own_part]
            dq_acc[...] += lax.dot_general(
                key_list[rows], ds_low, (((0,), (0,)), ((), ())), preferred_element_type=F32
            )
            return jnp.maximum(ds_now, jnp.max(jnp.abs(dscores), axis=0, keepdims=True))

        ds_top = lax.fori_loop(0, steps, grad_step, ds_top)
        cosine = rope[half, :, :head_dim]
        signed_sine = rope[half, :, head_dim:]
        grad_q = dq_acc[...].T * scale
        for head in range(heads):
            part = grad_q[head * span_len : (head + 1) * span_len]
            gq_ref[own, pl.ds(head * head_dim, head_dim)] = unrotate(part, cosine, signed_sine).astype(BF16)

    extra = spread_max(jnp.max(out_top[...]), jnp.max(ds_top), 2 * head_dim)
    for index in range(shards):
        rows = pl.ds(pl.multiple_of((me ^ index) * tok_dev, tok_dev), tok_dev)
        target = (keep_ref, send_ref)[index % 2]
        kind = target.dtype
        target[index // 2, :tok_dev, :head_dim] = dk_acc[rows].astype(kind)
        target[index // 2, :tok_dev, head_dim:] = dv_acc[rows].astype(kind)
        target[index // 2, tok_dev:] = extra.astype(kind)


def merge_kernel(keep_ref, got_ref, next_ref, send_ref):
    tok_dev = keep_ref.shape[1] - EXTRA
    extra = join_max([keep_ref[0, tok_dev:], got_ref[0, tok_dev:]])
    for index in range(keep_ref.shape[0]):
        both = keep_ref[index, :tok_dev] + got_ref[index, :tok_dev].astype(F32)
        target = (next_ref, send_ref)[index % 2]
        target[index // 2, :tok_dev] = both.astype(target.dtype)
        target[index // 2, tok_dev:] = extra.astype(target.dtype)


def finish_kernel(rope, gq_ref, keep_ref, got_ref, rows_ref, gkv_ref):
    tok_dev, width = gq_ref.shape
    head_dim = keep_ref.shape[2] // 2
    total = keep_ref[0, :tok_dev] + got_ref[0, :tok_dev].astype(F32)
    extra = join_max([keep_ref[0, tok_dev:], got_ref[0, tok_dev:]])
    wide = rope[...].reshape(tok_dev, 2 * head_dim)
    grad_k = unrotate(
        total[:, :head_dim] * (1.0 / math.sqrt(head_dim)), wide[:, :head_dim], wide[:, head_dim:]
    ).astype(BF16)
    grad_v = total[:, head_dim:].astype(BF16)
    gkv_ref[:tok_dev, :head_dim] = grad_k
    gkv_ref[:tok_dev, head_dim:] = grad_v
    gkv_ref[tok_dev:] = extra.astype(BF16)
    rows_ref[:, :width] = gq_ref[...]
    rows_ref[:, width : width + head_dim] = grad_k
    rows_ref[:, width + head_dim :] = grad_v


def partial_kernel(count, groups, blocks, tile, adds, *refs):
    xs, gs = refs[: groups * count], refs[groups * count : (groups + 1) * count]
    rest = refs[(groups + 1) * count :]
    tok_dev = xs[0].shape[0]
    for index in range(blocks * groups):
        block, group = index // groups, index % groups
        cols = slice(block * tile, (block + 1) * tile)
        total = None
        for x_ref, g_ref in zip(xs[group * count : (group + 1) * count], gs):
            term = lax.dot_general(
                x_ref[:, cols], g_ref[:tok_dev], (((0,), (0,)), ((), ())), preferred_element_type=F32
            )
            total = term if total is None else total + term
        rows = slice(index * tile, (index + 1) * tile)
        if adds:
            total = total + rest[0][rows].astype(F32)
            target = rest[1 + block % 2]
            place = block // 2 * groups + group
            target[place * tile : (place + 1) * tile] = total.astype(target.dtype)
        else:
            rest[0][rows] = total.astype(BF16)


def total_kernel(places, *refs):
    out_ref, amax_ref = refs[-2:]
    used = 0
    for (rows, cols), count in places:
        total = refs[used][: rows.stop - rows.start]
        for ref in refs[used + 1 : used + count]:
            total = total + ref[: rows.stop - rows.start].astype(F32)
        out_ref[rows, cols] = total
        used += count
    maxima = [ref[ref.shape[0] - EXTRA :] for ref in refs[used:-2]]
    out_max, ds_max = read_max(join_max(maxima))
    lane = lax.broadcasted_iota(jnp.int32, (1, 2), 1)
    amax_ref[0] = jnp.where(lane == 0, out_max[:, :2], ds_max[:, :2])


def start_packing(replicas, shards, order, rest, refs, sems):
    rep, me = lax.axis_index("dp"), lax.axis_index("context")
    places = [(1, place, place - shards // 2) for place in range(shards // 2, shards)]
    if not rest:
        places = [(0, place, place) for place in range(shards)]
        places += [(1, place, shards + place) for place in range(shards // 2)]
    tile = refs[1].shape[1] // len(places)
    copies = []
    for step in range(replicas):
        for index, (part, place, spot) in enumerate(places):
            source = ((((rep ^ step) * shards) + (me ^ order[place])) * 2 + part) * tile
            copy = pltpu.make_async_copy(
                refs[0].at[:, pl.ds(pl.multiple_of(source, tile), tile)],
                refs[1 + step].at[:, pl.ds(spot * tile, tile)],
                sems.at[step, index],
            )
            copy.start()
            copies.append(copy)
    return copies


def prepare_kernel(replicas, shards, order, pair_ref, docs_ref, k_ref, v_ref, table_ref, q_ref, g_ref, *refs):
    rope_sems, sems, x_sems, q_buf, g_buf = refs[-5:]
    x_refs, outs = refs[:-12], refs[-12:-5]
    list_ref, kv_ref, bounds_ref, top_ref, rope_ref, q_cat, g_cat = outs
    x_copies = []
    if x_refs:
        x_copies = start_packing(replicas, shards, order, False, x_refs[: 1 + replicas], x_sems.at[0])
        rest_refs = (x_refs[0],) + tuple(x_refs[1 + replicas :])
        x_copies += start_packing(replicas, shards, order, True, rest_refs, x_sems.at[1])
    kv_ref[:, : k_ref.shape[1]] = k_ref[...]
    kv_ref[:, k_ref.shape[1] :] = v_ref[...]
    waits = [pltpu.make_async_copy(q_ref, q_buf, sems.at[0]), pltpu.make_async_copy(g_ref, g_buf, sems.at[1])]
    for copy in waits:
        copy.start()
    tok_dev = q_ref.shape[0]
    span_len = tok_dev // 2
    lanes, head_dim = q_cat.shape[1:]
    me = lax.axis_index("context")
    pair = pair_ref[me]
    copies = []
    for half in range(2):
        start = pl.multiple_of(span_of(pair, half, shards) * span_len, 8)
        copy = pltpu.make_async_copy(table_ref.at[pl.ds(start, span_len)], rope_ref.at[half], rope_sems.at[half])
        copy.start()
        copies.append(copy)
    docs = docs_ref[...]
    starts = [jnp.sum(jnp.where(docs < value, 1.0, 0.0)) for value in range(1, DOC_VALUES)]
    lane_row = lax.broadcasted_iota(jnp.int32, (1, lanes), 1) % span_len
    for half in range(2):
        span = span_of(pair, half, shards)
        base = span * span_len
        base_f = base.astype(F32)
        first_start = jnp.float32(0.0)
        for start in starts:
            first_start = jnp.maximum(first_start, jnp.where(start <= base_f, start, 0.0))
        first_key = first_start.astype(jnp.int32)

        def listing(block, count):
            other = pair_ref[block // 2]
            key_span = jnp.where(block % 2 == 0, other, 2 * shards - 1 - other)
            list_ref[half, 0, count] = block
            list_ref[half, 1, count] = key_span
            needed = (key_span <= span) & (key_span * span_len + span_len > first_key)
            return count + needed.astype(jnp.int32)

        count = lax.fori_loop(0, 2 * shards, listing, jnp.int32(0))
        list_ref[half, 2, 0] = count
        list_ref[half, 0, count] = 2 * shards
        list_ref[half, 1, count] = 2 * shards
        query_pos = base + lane_row
        query_f = query_pos.astype(F32)
        doc_start = jnp.zeros((1, lanes), F32)
        for start in starts:
            doc_start = jnp.maximum(doc_start, jnp.where(start <= query_f, start, 0.0))
        bounds_ref[half, 0:1] = doc_start.astype(jnp.int32)
        bounds_ref[half, 1:2] = query_pos
    waits[0].wait()
    waits[1].wait()
    for half in range(2):
        own = slice(half * span_len, (half + 1) * span_len)
        for head in range(q_ref.shape[1] // head_dim):
            rows = slice(head * span_len, (head + 1) * span_len)
            cols = slice(head * head_dim, (head + 1) * head_dim)
            q_cat[half, rows] = q_buf[own, cols]
            g_cat[half, rows] = g_buf[own, cols]
    top_ref[...] = jnp.max(jnp.abs(g_cat[...].astype(F32)).reshape(-1, 8, head_dim), axis=0)
    for copy in copies + x_copies:
        copy.wait()


def params(mebibytes):
    return pltpu.CompilerParams(vmem_limit_bytes=mebibytes << 20)


def cost(microseconds):
    return pl.CostEstimate(flops=int(microseconds * 1.0e6), bytes_accessed=0, transcendentals=0)


def local(query_rows, key_rows, value_rows, out_grads, layer_input, doc_ids, pair_span):
    shards = lax.axis_size("context")
    replicas = lax.axis_size("dp")
    tok_dev = query_rows.shape[1]
    head_dim = key_rows.shape[2]
    width = query_rows.shape[2]
    heads = width // head_dim
    model_width = layer_input.shape[2]
    span_len = tok_dev // 2
    seq_len = tok_dev * shards
    qkv_width = width + 2 * head_dim
    lanes = heads * span_len
    slice_rows = model_width // (replicas * shards)
    tile = slice_rows // 2
    packs = tile % 128 == 0
    half_shards = shards // 2
    table = jnp.asarray(rope_tables(seq_len, head_dim))
    order = list(range(1, shards, 2)) + list(range(0, shards, 2))

    def context_move(x, step):
        return lax.ppermute(x, "context", [(i, i ^ step) for i in range(shards)])

    def dp_move(x, step):
        return lax.ppermute(x, "dp", [(i, i ^ step) for i in range(replicas)])

    def struct(shape, kind=BF16):
        return jax.ShapeDtypeStruct(shape, kind)

    outs = [
        struct((2, 3, 2 * shards + 1), jnp.int32),
        struct((tok_dev, 2 * head_dim)),
        struct((2, 2, lanes), jnp.int32),
        struct((8, head_dim), F32),
        struct((2, span_len, 2 * head_dim), F32),
        struct((2, lanes, head_dim)),
        struct((2, lanes, head_dim)),
    ]
    if packs:
        outs = [struct((tok_dev, count * tile)) for count in (shards + half_shards, half_shards) for _ in range(replicas)] + outs
    prepared = pl.pallas_call(
        functools.partial(prepare_kernel, replicas, shards, order),
        out_shape=outs,
        in_specs=[SMEM] + [VMEM] * 3 + [ANY] * (3 + packs),
        out_specs=[VMEM] * (len(outs) - 7) + [SMEM] + [VMEM] * 6,
        scratch_shapes=[
            pltpu.SemaphoreType.DMA((2,)),
            pltpu.SemaphoreType.DMA((2,)),
            pltpu.SemaphoreType.DMA((2, replicas, shards + half_shards)),
            pltpu.VMEM((tok_dev, width), BF16),
            pltpu.VMEM((tok_dev, width), BF16),
        ],
        compiler_params=params(60),
        cost_estimate=cost(4),
        name="prepare",
    )(pair_span, doc_ids, key_rows[0], value_rows[0], table, query_rows[0], out_grads[0], *([layer_input[0]] if packs else []))
    order_list, own_kv, bounds, out_top, rope, q_cats, g_cats = prepared[-7:]
    if packs:
        x_most, x_rest = list(prepared[:replicas]), list(prepared[replicas : 2 * replicas])
    else:
        me, rep = lax.axis_index("context"), lax.axis_index("dp")
        x_most, x_rest = [], []
        for step in range(replicas):
            part = lax.dynamic_slice_in_dim(layer_input[0], (rep ^ step) * shards * slice_rows, shards * slice_rows, 1)
            part = jnp.take(part.reshape(tok_dev, shards, 2, tile), jnp.asarray(order, jnp.int32) ^ me, axis=1)
            most = jnp.concatenate([part[:, :, 0], part[:, :half_shards, 1]], axis=1)
            x_most.append(most.reshape(tok_dev, -1))
            x_rest.append(part[:, half_shards:, 1].reshape(tok_dev, -1))

    def tie(value, *others):
        return lax.optimization_barrier((value, others))[0]

    def exchange(parts):
        return [parts[0]] + [dp_move(parts[step], step) for step in range(1, replicas)]

    x_most = exchange(x_most)
    kv_all = lax.all_gather(own_kv, "context", axis=0, tiled=True)

    buf = (shards + 1, 2 * span_len, lanes)
    padded = (seq_len + 2 * span_len, head_dim)
    grad_q, keep, send = pl.pallas_call(
        functools.partial(attend_kernel, shards, heads),
        out_shape=[
            struct((tok_dev, width)),
            struct((shards // 2, tok_dev + EXTRA, 2 * head_dim), F32),
            struct((shards // 2, tok_dev + EXTRA, 2 * head_dim)),
        ],
        in_specs=[SMEM] + [VMEM] * 6,
        out_specs=[VMEM] * 3,
        scratch_shapes=[
            pltpu.VMEM(padded, BF16),
            pltpu.VMEM(padded, BF16),
            pltpu.VMEM(buf, F32),
            pltpu.VMEM(buf, F32),
            pltpu.VMEM((head_dim, lanes), F32),
            pltpu.VMEM(padded, F32),
            pltpu.VMEM(padded, F32),
        ],
        compiler_params=params(60),
        cost_estimate=cost(12),
        name="attend",
    )(order_list, rope, bounds, out_top, q_cats, g_cats, kv_all)

    grad_q, send = tie((grad_q, send), x_most)
    gq = exchange([grad_q] * replicas)

    block = (tok_dev + EXTRA, 2 * head_dim)
    got, step = context_move(send, 1), 2
    while step < shards:
        count = shards // 2 // step
        keep, send = pl.pallas_call(
            merge_kernel,
            out_shape=[struct((count,) + block, F32), struct((count,) + block)],
            in_specs=[VMEM] * 2,
            out_specs=[VMEM] * 2,
            compiler_params=params(8),
        cost_estimate=cost(2),
            name="merge_rows",
        )(keep, got)
        got, step = context_move(send, step), step * 2

    def partial_weights(groups, gs, arrived=None):
        parts = [x for _, xs in groups for x in xs]
        block = (tok_dev, half_shards * tile)
        specs = [pl.BlockSpec(block, lambda i, first=first: (0, first)) for first, xs in groups for _ in xs]
        rows, cols = half_shards * len(groups) * tile, gs[0].shape[1]
        adds = arrived is not None
        out_shape = [struct((rows, cols))]
        if adds:
            out_shape = [struct((rows // 2, cols), F32), struct((rows // 2, cols))]
        result = pl.pallas_call(
            functools.partial(partial_kernel, replicas, len(groups), half_shards, tile, adds),
            out_shape=out_shape,
            grid=(1,),
            in_specs=specs + [VMEM] * (replicas + adds),
            out_specs=[VMEM] * len(out_shape),
            compiler_params=params(16),
            cost_estimate=cost(2),
            name="weights_own_core" if adds else "weights_other_core",
        )(*parts, *gs, *([arrived] if adds else []))
        return result if adds else result[0]

    def split_blocks(x, rows):
        parts = x.reshape(-1, 2, rows, x.shape[1])
        return parts[:, 0].reshape(-1, x.shape[1]), parts[:, 1].reshape(-1, x.shape[1])

    def next_terms(kept, got, rows):
        kept_even, kept_odd = split_blocks(kept, rows)
        got_even, got_odd = split_blocks(got, rows)
        return kept_even + got_even.astype(F32), (kept_odd + got_odd.astype(F32)).astype(BF16)

    def last_steps(kept, got, rows):
        terms, step, sent = [kept, got], 4, got
        while step < shards:
            kept, sent = next_terms(kept, got, rows)
            got, step = context_move(sent, step), step * 2
            terms.append(got)
        return terms, sent

    gq = tie(gq, keep, got)
    away = partial_weights([(0, x_most)], gq)
    arrived = context_move(away, 1)
    keep, got = tie((keep, got), away)
    grad_rows, grad_kv = pl.pallas_call(
        finish_kernel,
        out_shape=[struct((tok_dev, qkv_width)), struct(block)],
        in_specs=[VMEM] * 4,
        out_specs=[VMEM] * 2,
        compiler_params=params(8),
        cost_estimate=cost(2),
        name="finish_rows",
    )(rope, grad_q, keep, got)
    x_rest = exchange(tie(x_rest, gq))
    gkv = exchange([grad_kv] * replicas)
    kept, sent = partial_weights([(1, x_most)], gq, tie(arrived, grad_kv))
    first = kept, context_move(sent, 2)
    away = partial_weights([(2, tie(x_most, sent))], gq)
    arrived = context_move(away, 1)
    first, sent = last_steps(*first, tile)
    kept, sent = partial_weights([(0, x_rest)], gq, tie(arrived, sent))
    second = kept, context_move(sent, 2)
    away = partial_weights([(0, x_most), (2, x_most)], tie(gkv, sent, first))
    arrived = context_move(away, 1)
    second, sent = last_steps(*second, tile)
    kept, sent = partial_weights([(1, x_most), (0, x_rest)], gkv, tie(arrived, sent))
    third = last_steps(kept, context_move(sent, 2), 2 * tile)[0]
    terms = [first, second, third]
    upper, lower, full = slice(0, tile), slice(tile, 2 * tile), slice(0, width)
    spots = [(upper, full), (lower, full), (slice(0, 2 * tile), slice(width, qkv_width))]
    places = [(spot, len(part)) for spot, part in zip(spots, terms)]
    grad_weight, amax = pl.pallas_call(
        functools.partial(total_kernel, places),
        out_shape=[struct((slice_rows, qkv_width), F32), struct((1, 1, 2), F32)],
        in_specs=[VMEM] * (sum(len(part) for part in terms) + replicas),
        out_specs=[VMEM] * 2,
        compiler_params=params(16),
        name="total_weights",
    )(*[x for part in terms for x in part], *gkv)
    return (grad_rows[None], grad_weight, amax)


def solution(mesh):
    in_specs = (
        P("dp", "context", None),
        P("dp", "context", None),
        P("dp", "context", None),
        P("dp", "context", None),
        P("dp", "context", None),
        P("dp", None),
        P(),
    )
    out_specs = (P("dp", "context", None), P(("dp", "context"), None), P("dp", "context", None))
    return jax.shard_map(local, mesh=mesh, in_specs=in_specs, out_specs=out_specs, check_vma=False)
```

```python
import functools
import math

import jax
import jax.numpy as jnp
import numpy as np
from jax import lax
from jax.experimental import pallas as pl
from jax.experimental.pallas import tpu as pltpu
from jax.sharding import PartitionSpec as P

THETA_BASE = 500000.0
NEG_LARGE = -1e30
DOC_VALUES = 8
EXTRA = 16
GROUP = 3
F32 = jnp.float32
BF16 = jnp.bfloat16
VMEM = pl.BlockSpec(memory_space=pltpu.VMEM)
SMEM = pl.BlockSpec(memory_space=pltpu.SMEM)
ANY = pl.BlockSpec(memory_space=pl.ANY)


def rope_tables(seq_len, head_dim):
    inverse_freq = THETA_BASE ** (-2.0 * np.arange(head_dim // 2) / head_dim)
    angles = np.arange(seq_len)[:, None] * inverse_freq[None, :]
    angles = np.concatenate([angles, angles], axis=1)
    sign = np.where(np.arange(head_dim) < head_dim // 2, 1.0, -1.0)
    return np.concatenate(
        [np.cos(angles).astype(np.float32), (np.sin(angles) * sign).astype(np.float32)], axis=1
    )


def unrotate(rows, cosine, signed_sine):
    return rows * cosine + pltpu.roll(rows, rows.shape[-1] // 2, 1) * signed_sine


def span_of(pair, half, shards):
    return pair if half == 0 else 2 * shards - 1 - pair


def spread_max(out_max, ds_max, width):
    high = ds_max.astype(BF16).astype(F32)
    middle = (ds_max - high).astype(BF16).astype(F32)
    low = ds_max - high - middle
    row = lax.broadcasted_iota(jnp.int32, (EXTRA, width), 0)
    return jnp.where(
        row == 0,
        out_max,
        jnp.where(row == 1, high, jnp.where(row == 2, middle, jnp.where(row == 3, low, 0.0))),
    )


def read_max(rows):
    wide = rows.astype(F32)
    return wide[0:1], wide[1:2] + wide[2:3] + wide[3:4]


def join_max(parts):
    pairs = [read_max(part) for part in parts]
    out_max, ds_max = pairs[0]
    for other_out, other_ds in pairs[1:]:
        out_max, ds_max = jnp.maximum(out_max, other_out), jnp.maximum(ds_max, other_ds)
    return spread_max(out_max, ds_max, parts[0].shape[1])


def attend_kernel(shards, heads, order, rope, bounds, out_top, q_cats, g_cats, kv_ref, *refs):
    gq_ref, keep_ref, send_ref, key_list, value_list, score_buf, dprob_buf, dq_acc, dk_acc, dv_acc = refs
    lanes, head_dim = q_cats.shape[1:]
    span_len = lanes // heads
    tok_dev = 2 * span_len
    scale = 1.0 / math.sqrt(head_dim)
    me = lax.axis_index("context")
    dk_acc[...] = jnp.zeros_like(dk_acc)
    dv_acc[...] = jnp.zeros_like(dv_acc)
    ds_top = jnp.zeros((1, lanes), F32)
    sub = lax.broadcasted_iota(jnp.int32, (GROUP * span_len, 1), 0)

    for half in range(2):
        count = order[half, 2, 0]
        steps = (count + GROUP - 1) // GROUP

        def listing(index, unused):
            source = pl.ds(pl.multiple_of(order[half, 0, index] * span_len, span_len), span_len)
            target = pl.ds(pl.multiple_of(index * span_len, span_len), span_len)
            key_list[target] = kv_ref[source, :head_dim]
            value_list[target] = kv_ref[source, head_dim:]
            return unused

        lax.fori_loop(0, count, listing, 0)
        spare = pl.ds(pl.multiple_of(count * span_len, span_len), (GROUP - 1) * span_len)
        key_list[spare] = jnp.zeros(((GROUP - 1) * span_len, head_dim), BF16)
        value_list[spare] = jnp.zeros(((GROUP - 1) * span_len, head_dim), BF16)
        doc_first = bounds[half, 0:1]
        query_pos = bounds[half, 1:2]
        own = pl.ds(half * span_len, span_len)
        q_cat, g_cat = q_cats.at[half], g_cats.at[half]

        def score_step(index, top):
            rows = pl.ds(pl.multiple_of(index * GROUP * span_len, span_len), GROUP * span_len)
            start = order[half, 1, GROUP * index + GROUP - 1] - (GROUP - 1)
            for part in range(GROUP - 2, -1, -1):
                start = jnp.where(sub < (part + 1) * span_len, order[half, 1, GROUP * index + part] - part, start)
            key_pos = start * span_len + sub
            scores = lax.dot_general(
                key_list[rows], q_cat[...], (((1,), (1,)), ((), ())), preferred_element_type=F32
            )
            allowed = (key_pos <= query_pos) & (key_pos >= doc_first)
            scores = jnp.where(allowed, scores, NEG_LARGE)
            score_buf[index] = scores
            dprob_buf[index] = lax.dot_general(
                value_list[rows], g_cat[...], (((1,), (1,)), ((), ())), preferred_element_type=F32
            )
            return jnp.maximum(top, jnp.max(scores, axis=0, keepdims=True))

        top = lax.fori_loop(0, steps, score_step, jnp.full((1, lanes), NEG_LARGE, F32))

        def exp_step(index, sums):
            total, weighted = sums
            expd = jnp.exp((score_buf[index] - top) * scale)
            score_buf[index] = expd
            return (
                total + jnp.sum(expd, axis=0, keepdims=True),
                weighted + jnp.sum(expd * dprob_buf[index], axis=0, keepdims=True),
            )

        zero_row = jnp.zeros((1, lanes), F32)
        total, weighted = lax.fori_loop(0, steps, exp_step, (zero_row, zero_row))
        inverse = 1.0 / total
        delta = weighted * inverse
        dq_acc[...] = jnp.zeros_like(dq_acc)

        def grad_step(index, ds_now):
            rows = pl.ds(pl.multiple_of(index * GROUP * span_len, span_len), GROUP * span_len)
            probs = score_buf[index] * inverse
            dscores = probs * (dprob_buf[index] - delta)
            probs_low = probs.astype(BF16)
            ds_low = dscores.astype(BF16)
            grad_v = jnp.dot(probs_low, g_cat[...], preferred_element_type=F32)
            grad_k = jnp.dot(ds_low, q_cat[...], preferred_element_type=F32)
            for part in range(GROUP):
                block = pl.ds(pl.multiple_of(order[half, 0, GROUP * index + part] * span_len, span_len), span_len)
                own_part = slice(part * span_len, (part + 1) * span_len)
                dv_acc[block] += grad_v[own_part]
                dk_acc[block] += grad_k[own_part]
            dq_acc[...] += lax.dot_general(
                key_list[rows], ds_low, (((0,), (0,)), ((), ())), preferred_element_type=F32
            )
            return jnp.maximum(ds_now, jnp.max(jnp.abs(dscores), axis=0, keepdims=True))

        ds_top = lax.fori_loop(0, steps, grad_step, ds_top)
        cosine = rope[half, :, :head_dim]
        signed_sine = rope[half, :, head_dim:]
        grad_q = dq_acc[...].T * scale
        for head in range(heads):
            part = grad_q[head * span_len : (head + 1) * span_len]
            gq_ref[own, pl.ds(head * head_dim, head_dim)] = unrotate(part, cosine, signed_sine).astype(BF16)

    extra = spread_max(jnp.max(out_top[...]), jnp.max(ds_top), 2 * head_dim)
    for index in range(shards):
        rows = pl.ds(pl.multiple_of((me ^ index) * tok_dev, tok_dev), tok_dev)
        target = (keep_ref, send_ref)[index % 2]
        kind = target.dtype
        target[index // 2, :tok_dev, :head_dim] = dk_acc[rows].astype(kind)
        target[index // 2, :tok_dev, head_dim:] = dv_acc[rows].astype(kind)
        target[index // 2, tok_dev:] = extra.astype(kind)


def merge_kernel(keep_ref, got_ref, next_ref, send_ref):
    tok_dev = keep_ref.shape[1] - EXTRA
    extra = join_max([keep_ref[0, tok_dev:], got_ref[0, tok_dev:]])
    for index in range(keep_ref.shape[0]):
        both = keep_ref[index, :tok_dev] + got_ref[index, :tok_dev].astype(F32)
        target = (next_ref, send_ref)[index % 2]
        target[index // 2, :tok_dev] = both.astype(target.dtype)
        target[index // 2, tok_dev:] = extra.astype(target.dtype)


def finish_kernel(rope, gq_ref, keep_ref, got_ref, rows_ref, gkv_ref):
    tok_dev, width = gq_ref.shape
    head_dim = keep_ref.shape[2] // 2
    total = keep_ref[0, :tok_dev] + got_ref[0, :tok_dev].astype(F32)
    extra = join_max([keep_ref[0, tok_dev:], got_ref[0, tok_dev:]])
    wide = rope[...].reshape(tok_dev, 2 * head_dim)
    grad_k = unrotate(
        total[:, :head_dim] * (1.0 / math.sqrt(head_dim)), wide[:, :head_dim], wide[:, head_dim:]
    ).astype(BF16)
    grad_v = total[:, head_dim:].astype(BF16)
    gkv_ref[:tok_dev, :head_dim] = grad_k
    gkv_ref[:tok_dev, head_dim:] = grad_v
    gkv_ref[tok_dev:] = extra.astype(BF16)
    rows_ref[:, :width] = gq_ref[...]
    rows_ref[:, width : width + head_dim] = grad_k
    rows_ref[:, width + head_dim :] = grad_v


def partial_kernel(count, groups, blocks, tile, adds, *refs):
    xs, gs = refs[: groups * count], refs[groups * count : (groups + 1) * count]
    rest = refs[(groups + 1) * count :]
    tok_dev = xs[0].shape[0]
    for index in range(blocks * groups):
        block, group = index // groups, index % groups
        cols = slice(block * tile, (block + 1) * tile)
        total = None
        for x_ref, g_ref in zip(xs[group * count : (group + 1) * count], gs):
            term = lax.dot_general(
                x_ref[:, cols], g_ref[:tok_dev], (((0,), (0,)), ((), ())), preferred_element_type=F32
            )
            total = term if total is None else total + term
        rows = slice(index * tile, (index + 1) * tile)
        if adds:
            total = total + rest[0][rows].astype(F32)
            target = rest[1 + block % 2]
            place = block // 2 * groups + group
            target[place * tile : (place + 1) * tile] = total.astype(target.dtype)
        else:
            rest[0][rows] = total.astype(BF16)


def total_kernel(places, *refs):
    out_ref, amax_ref = refs[-2:]
    used = 0
    for (rows, cols), count in places:
        total = refs[used][: rows.stop - rows.start]
        for ref in refs[used + 1 : used + count]:
            total = total + ref[: rows.stop - rows.start].astype(F32)
        out_ref[rows, cols] = total
        used += count
    maxima = [ref[ref.shape[0] - EXTRA :] for ref in refs[used:-2]]
    out_max, ds_max = read_max(join_max(maxima))
    lane = lax.broadcasted_iota(jnp.int32, (1, 2), 1)
    amax_ref[0] = jnp.where(lane == 0, out_max[:, :2], ds_max[:, :2])


def start_packing(replicas, shards, order, rest, refs, sems):
    rep, me = lax.axis_index("dp"), lax.axis_index("context")
    places = [(1, place, place - shards // 2) for place in range(shards // 2, shards)]
    if not rest:
        places = [(0, place, place) for place in range(shards)]
        places += [(1, place, shards + place) for place in range(shards // 2)]
    tile = refs[1].shape[1] // len(places)
    copies = []
    for step in range(replicas):
        for index, (part, place, spot) in enumerate(places):
            source = ((((rep ^ step) * shards) + (me ^ order[place])) * 2 + part) * tile
            copy = pltpu.make_async_copy(
                refs[0].at[:, pl.ds(pl.multiple_of(source, tile), tile)],
                refs[1 + step].at[:, pl.ds(spot * tile, tile)],
                sems.at[step, index],
            )
            copy.start()
            copies.append(copy)
    return copies


def pack_rest_kernel(replicas, shards, order, *refs):
    for copy in start_packing(replicas, shards, order, True, refs[:-1], refs[-1]):
        copy.wait()


def prepare_kernel(replicas, shards, order, pair_ref, docs_ref, k_ref, v_ref, table_ref, q_ref, g_ref, *refs):
    rope_sems, sems, x_sems, q_buf, g_buf = refs[-5:]
    x_refs, outs = refs[:-12], refs[-12:-5]
    list_ref, kv_ref, bounds_ref, top_ref, rope_ref, q_cat, g_cat = outs
    x_copies = []
    if x_refs:
        x_copies = start_packing(replicas, shards, order, False, x_refs, x_sems)
    kv_ref[:, : k_ref.shape[1]] = k_ref[...]
    kv_ref[:, k_ref.shape[1] :] = v_ref[...]
    waits = [pltpu.make_async_copy(q_ref, q_buf, sems.at[0]), pltpu.make_async_copy(g_ref, g_buf, sems.at[1])]
    for copy in waits:
        copy.start()
    tok_dev = q_ref.shape[0]
    span_len = tok_dev // 2
    lanes, head_dim = q_cat.shape[1:]
    me = lax.axis_index("context")
    pair = pair_ref[me]
    copies = []
    for half in range(2):
        start = pl.multiple_of(span_of(pair, half, shards) * span_len, 8)
        copy = pltpu.make_async_copy(table_ref.at[pl.ds(start, span_len)], rope_ref.at[half], rope_sems.at[half])
        copy.start()
        copies.append(copy)
    docs = docs_ref[...]
    starts = [jnp.sum(jnp.where(docs < value, 1.0, 0.0)) for value in range(1, DOC_VALUES)]
    lane_row = lax.broadcasted_iota(jnp.int32, (1, lanes), 1) % span_len
    for half in range(2):
        span = span_of(pair, half, shards)
        base = span * span_len
        base_f = base.astype(F32)
        first_start = jnp.float32(0.0)
        for start in starts:
            first_start = jnp.maximum(first_start, jnp.where(start <= base_f, start, 0.0))
        first_key = first_start.astype(jnp.int32)

        def listing(block, count):
            other = pair_ref[block // 2]
            key_span = jnp.where(block % 2 == 0, other, 2 * shards - 1 - other)
            list_ref[half, 0, count] = block
            list_ref[half, 1, count] = key_span
            needed = (key_span <= span) & (key_span * span_len + span_len > first_key)
            return count + needed.astype(jnp.int32)

        count = lax.fori_loop(0, 2 * shards, listing, jnp.int32(0))
        list_ref[half, 2, 0] = count
        for spare in range(GROUP - 1):
            list_ref[half, 0, count + spare] = 2 * shards
            list_ref[half, 1, count + spare] = 2 * shards
        query_pos = base + lane_row
        query_f = query_pos.astype(F32)
        doc_start = jnp.zeros((1, lanes), F32)
        for start in starts:
            doc_start = jnp.maximum(doc_start, jnp.where(start <= query_f, start, 0.0))
        bounds_ref[half, 0:1] = doc_start.astype(jnp.int32)
        bounds_ref[half, 1:2] = query_pos
    waits[0].wait()
    waits[1].wait()
    for half in range(2):
        own = slice(half * span_len, (half + 1) * span_len)
        for head in range(q_ref.shape[1] // head_dim):
            rows = slice(head * span_len, (head + 1) * span_len)
            cols = slice(head * head_dim, (head + 1) * head_dim)
            q_cat[half, rows] = q_buf[own, cols]
            g_cat[half, rows] = g_buf[own, cols]
    top_ref[...] = jnp.max(jnp.abs(g_cat[...].astype(F32)).reshape(-1, 8, head_dim), axis=0)
    for copy in copies + x_copies:
        copy.wait()


def params(mebibytes):
    return pltpu.CompilerParams(vmem_limit_bytes=mebibytes << 20)


def cost(microseconds):
    return pl.CostEstimate(flops=int(microseconds * 1.0e6), bytes_accessed=0, transcendentals=0)


def local(query_rows, key_rows, value_rows, out_grads, layer_input, doc_ids, pair_span):
    shards = lax.axis_size("context")
    replicas = lax.axis_size("dp")
    tok_dev = query_rows.shape[1]
    head_dim = key_rows.shape[2]
    width = query_rows.shape[2]
    heads = width // head_dim
    model_width = layer_input.shape[2]
    span_len = tok_dev // 2
    seq_len = tok_dev * shards
    qkv_width = width + 2 * head_dim
    lanes = heads * span_len
    slice_rows = model_width // (replicas * shards)
    tile = slice_rows // 2
    packs = tile % 128 == 0
    half_shards = shards // 2
    table = jnp.asarray(rope_tables(seq_len, head_dim))
    order = list(range(1, shards, 2)) + list(range(0, shards, 2))

    def context_move(x, step):
        return lax.ppermute(x, "context", [(i, i ^ step) for i in range(shards)])

    def dp_move(x, step):
        return lax.ppermute(x, "dp", [(i, i ^ step) for i in range(replicas)])

    def struct(shape, kind=BF16):
        return jax.ShapeDtypeStruct(shape, kind)

    outs = [
        struct((2, 3, 2 * shards + GROUP), jnp.int32),
        struct((tok_dev, 2 * head_dim)),
        struct((2, 2, lanes), jnp.int32),
        struct((8, head_dim), F32),
        struct((2, span_len, 2 * head_dim), F32),
        struct((2, lanes, head_dim)),
        struct((2, lanes, head_dim)),
    ]
    if packs:
        outs = [struct((tok_dev, (shards + half_shards) * tile))] * replicas + outs
    prepared = pl.pallas_call(
        functools.partial(prepare_kernel, replicas, shards, order),
        out_shape=outs,
        in_specs=[SMEM] + [VMEM] * 3 + [ANY] * (3 + packs),
        out_specs=[VMEM] * (len(outs) - 7) + [SMEM] + [VMEM] * 6,
        scratch_shapes=[
            pltpu.SemaphoreType.DMA((2,)),
            pltpu.SemaphoreType.DMA((2,)),
            pltpu.SemaphoreType.DMA((replicas, shards + half_shards)),
            pltpu.VMEM((tok_dev, width), BF16),
            pltpu.VMEM((tok_dev, width), BF16),
        ],
        compiler_params=params(60),
        cost_estimate=cost(4),
        name="prepare",
    )(pair_span, doc_ids, key_rows[0], value_rows[0], table, query_rows[0], out_grads[0], *([layer_input[0]] if packs else []))
    order_list, own_kv, bounds, out_top, rope, q_cats, g_cats = prepared[-7:]
    if packs:
        x_most = list(prepared[:replicas])
    else:
        me, rep = lax.axis_index("context"), lax.axis_index("dp")
        x_most, x_rest = [], []
        for step in range(replicas):
            part = lax.dynamic_slice_in_dim(layer_input[0], (rep ^ step) * shards * slice_rows, shards * slice_rows, 1)
            part = jnp.take(part.reshape(tok_dev, shards, 2, tile), jnp.asarray(order, jnp.int32) ^ me, axis=1)
            most = jnp.concatenate([part[:, :, 0], part[:, :half_shards, 1]], axis=1)
            x_most.append(most.reshape(tok_dev, -1))
            x_rest.append(part[:, half_shards:, 1].reshape(tok_dev, -1))

    def tie(value, *others):
        return lax.optimization_barrier((value, others))[0]

    def exchange(parts):
        return [parts[0]] + [dp_move(parts[step], step) for step in range(1, replicas)]

    x_most = exchange(x_most)
    kv_all = lax.all_gather(own_kv, "context", axis=0, tiled=True)

    buf = ((2 * shards + GROUP - 1) // GROUP, GROUP * span_len, lanes)
    padded = (seq_len + GROUP * span_len, head_dim)
    grad_q, keep, send = pl.pallas_call(
        functools.partial(attend_kernel, shards, heads),
        out_shape=[
            struct((tok_dev, width)),
            struct((shards // 2, tok_dev + EXTRA, 2 * head_dim), F32),
            struct((shards // 2, tok_dev + EXTRA, 2 * head_dim)),
        ],
        in_specs=[SMEM] + [VMEM] * 6,
        out_specs=[VMEM] * 3,
        scratch_shapes=[
            pltpu.VMEM(padded, BF16),
            pltpu.VMEM(padded, BF16),
            pltpu.VMEM(buf, F32),
            pltpu.VMEM(buf, F32),
            pltpu.VMEM((head_dim, lanes), F32),
            pltpu.VMEM(padded, F32),
            pltpu.VMEM(padded, F32),
        ],
        compiler_params=params(60),
        cost_estimate=cost(12),
        name="attend",
    )(order_list, rope, bounds, out_top, q_cats, g_cats, kv_all)

    grad_q, send = tie((grad_q, send), x_most)
    gq = exchange([grad_q] * replicas)
    if packs:
        x_rest = pl.pallas_call(
            functools.partial(pack_rest_kernel, replicas, shards, order),
            out_shape=[struct((tok_dev, half_shards * tile))] * replicas,
            in_specs=[ANY],
            out_specs=[VMEM] * replicas,
            scratch_shapes=[pltpu.SemaphoreType.DMA((replicas, half_shards))],
            compiler_params=params(8),
            cost_estimate=cost(2),
            name="pack_rest",
        )(tie(layer_input[0], send))
        x_rest = list(x_rest)

    block = (tok_dev + EXTRA, 2 * head_dim)
    got, step = context_move(send, 1), 2
    while step < shards:
        count = shards // 2 // step
        keep, send = pl.pallas_call(
            merge_kernel,
            out_shape=[struct((count,) + block, F32), struct((count,) + block)],
            in_specs=[VMEM] * 2,
            out_specs=[VMEM] * 2,
            compiler_params=params(8),
        cost_estimate=cost(2),
            name="merge_rows",
        )(keep, got)
        got, step = context_move(send, step), step * 2

    def partial_weights(groups, gs, arrived=None):
        parts = [x for _, xs in groups for x in xs]
        block = (tok_dev, half_shards * tile)
        specs = [pl.BlockSpec(block, lambda i, first=first: (0, first)) for first, xs in groups for _ in xs]
        rows, cols = half_shards * len(groups) * tile, gs[0].shape[1]
        adds = arrived is not None
        out_shape = [struct((rows, cols))]
        if adds:
            out_shape = [struct((rows // 2, cols), F32), struct((rows // 2, cols))]
        result = pl.pallas_call(
            functools.partial(partial_kernel, replicas, len(groups), half_shards, tile, adds),
            out_shape=out_shape,
            grid=(1,),
            in_specs=specs + [VMEM] * (replicas + adds),
            out_specs=[VMEM] * len(out_shape),
            compiler_params=params(16),
            cost_estimate=cost(2),
            name="weights_own_core" if adds else "weights_other_core",
        )(*parts, *gs, *([arrived] if adds else []))
        return result if adds else result[0]

    def split_blocks(x, rows):
        parts = x.reshape(-1, 2, rows, x.shape[1])
        return parts[:, 0].reshape(-1, x.shape[1]), parts[:, 1].reshape(-1, x.shape[1])

    def next_terms(kept, got, rows):
        kept_even, kept_odd = split_blocks(kept, rows)
        got_even, got_odd = split_blocks(got, rows)
        return kept_even + got_even.astype(F32), (kept_odd + got_odd.astype(F32)).astype(BF16)

    def last_steps(kept, got, rows):
        terms, step, sent = [kept, got], 4, got
        while step < shards:
            kept, sent = next_terms(kept, got, rows)
            got, step = context_move(sent, step), step * 2
            terms.append(got)
        return terms, sent

    gq = tie(gq, keep, got, x_rest)
    away = partial_weights([(0, x_most)], gq)
    arrived = context_move(away, 1)
    keep, got = tie((keep, got), away)
    grad_rows, grad_kv = pl.pallas_call(
        finish_kernel,
        out_shape=[struct((tok_dev, qkv_width)), struct(block)],
        in_specs=[VMEM] * 4,
        out_specs=[VMEM] * 2,
        compiler_params=params(8),
        cost_estimate=cost(2),
        name="finish_rows",
    )(rope, grad_q, keep, got)
    x_rest = exchange(tie(x_rest, gq))
    gkv = exchange([grad_kv] * replicas)
    away = partial_weights([(2, tie(x_most, away))], gq)
    kept, sent = partial_weights([(1, x_most)], gq, tie(arrived, grad_kv, away))
    first = kept, context_move(sent, 2)
    arrived = context_move(away, 1)
    first, sent = last_steps(*first, tile)
    kept, sent = partial_weights([(0, x_rest)], gq, tie(arrived, sent))
    second = kept, context_move(sent, 2)
    away = partial_weights([(0, x_most), (2, x_most)], tie(gkv, sent, first))
    arrived = context_move(away, 1)
    second, sent = last_steps(*second, tile)
    kept, sent = partial_weights([(1, x_most), (0, x_rest)], gkv, tie(arrived, sent))
    third = last_steps(kept, context_move(sent, 2), 2 * tile)[0]
    terms = [first, second, third]
    upper, lower, full = slice(0, tile), slice(tile, 2 * tile), slice(0, width)
    spots = [(upper, full), (lower, full), (slice(0, 2 * tile), slice(width, qkv_width))]
    places = [(spot, len(part)) for spot, part in zip(spots, terms)]
    grad_weight, amax = pl.pallas_call(
        functools.partial(total_kernel, places),
        out_shape=[struct((slice_rows, qkv_width), F32), struct((1, 1, 2), F32)],
        in_specs=[VMEM] * (sum(len(part) for part in terms) + replicas),
        out_specs=[VMEM] * 2,
        compiler_params=params(16),
        name="total_weights",
    )(*[x for part in terms for x in part], *gkv)
    return (grad_rows[None], grad_weight, amax)


def solution(mesh):
    in_specs = (
        P("dp", "context", None),
        P("dp", "context", None),
        P("dp", "context", None),
        P("dp", "context", None),
        P("dp", "context", None),
        P("dp", None),
        P(),
    )
    out_specs = (P("dp", "context", None), P(("dp", "context"), None), P("dp", "context", None))
    return jax.shard_map(local, mesh=mesh, in_specs=in_specs, out_specs=out_specs, check_vma=False)
```

```python
import functools
import math

import jax
import jax.numpy as jnp
import numpy as np
from jax import lax
from jax.experimental import pallas as pl
from jax.experimental.pallas import tpu as pltpu
from jax.sharding import PartitionSpec as P

THETA_BASE = 500000.0
NEG_LARGE = -1e30
DOC_VALUES = 8
EXTRA = 16
GROUP = 3
F32 = jnp.float32
BF16 = jnp.bfloat16
VMEM = pl.BlockSpec(memory_space=pltpu.VMEM)
SMEM = pl.BlockSpec(memory_space=pltpu.SMEM)
ANY = pl.BlockSpec(memory_space=pl.ANY)


def rope_tables(seq_len, head_dim):
    inverse_freq = THETA_BASE ** (-2.0 * np.arange(head_dim // 2) / head_dim)
    angles = np.arange(seq_len)[:, None] * inverse_freq[None, :]
    angles = np.concatenate([angles, angles], axis=1)
    sign = np.where(np.arange(head_dim) < head_dim // 2, 1.0, -1.0)
    return np.concatenate(
        [np.cos(angles).astype(np.float32), (np.sin(angles) * sign).astype(np.float32)], axis=1
    )


def unrotate(rows, cosine, signed_sine):
    return rows * cosine + pltpu.roll(rows, rows.shape[-1] // 2, 1) * signed_sine


def span_of(pair, half, shards):
    return pair if half == 0 else 2 * shards - 1 - pair


def spread_max(out_max, ds_max, width):
    high = ds_max.astype(BF16).astype(F32)
    middle = (ds_max - high).astype(BF16).astype(F32)
    low = ds_max - high - middle
    row = lax.broadcasted_iota(jnp.int32, (EXTRA, width), 0)
    return jnp.where(
        row == 0,
        out_max,
        jnp.where(row == 1, high, jnp.where(row == 2, middle, jnp.where(row == 3, low, 0.0))),
    )


def read_max(rows):
    wide = rows.astype(F32)
    return wide[0:1], wide[1:2] + wide[2:3] + wide[3:4]


def join_max(parts):
    pairs = [read_max(part) for part in parts]
    out_max, ds_max = pairs[0]
    for other_out, other_ds in pairs[1:]:
        out_max, ds_max = jnp.maximum(out_max, other_out), jnp.maximum(ds_max, other_ds)
    return spread_max(out_max, ds_max, parts[0].shape[1])


def attend_kernel(shards, heads, order, rope, bounds, out_top, q_cats, g_cats, kv_ref, *refs):
    gq_ref, keep_ref, send_ref, key_list, value_list, score_buf, dprob_buf, dq_acc, dk_acc, dv_acc = refs
    lanes, head_dim = q_cats.shape[1:]
    span_len = lanes // heads
    tok_dev = 2 * span_len
    scale = 1.0 / math.sqrt(head_dim)
    me = lax.axis_index("context")
    dk_acc[...] = jnp.zeros_like(dk_acc)
    dv_acc[...] = jnp.zeros_like(dv_acc)
    ds_top = jnp.zeros((1, lanes), F32)
    sub = lax.broadcasted_iota(jnp.int32, (GROUP * span_len, 1), 0)

    for half in range(2):
        count = order[half, 2, 0]
        steps = (count + GROUP - 1) // GROUP

        def listing(index, unused):
            source = pl.ds(pl.multiple_of(order[half, 0, index] * span_len, span_len), span_len)
            target = pl.ds(pl.multiple_of(index * span_len, span_len), span_len)
            key_list[target] = kv_ref[source, :head_dim]
            value_list[target] = kv_ref[source, head_dim:]
            return unused

        lax.fori_loop(0, count, listing, 0)
        spare = pl.ds(pl.multiple_of(count * span_len, span_len), (GROUP - 1) * span_len)
        key_list[spare] = jnp.zeros(((GROUP - 1) * span_len, head_dim), BF16)
        value_list[spare] = jnp.zeros(((GROUP - 1) * span_len, head_dim), BF16)
        doc_first = bounds[half, 0:1]
        query_pos = bounds[half, 1:2]
        own = pl.ds(half * span_len, span_len)
        q_cat, g_cat = q_cats.at[half], g_cats.at[half]

        def score_step(index, top):
            rows = pl.ds(pl.multiple_of(index * GROUP * span_len, span_len), GROUP * span_len)
            start = order[half, 1, GROUP * index + GROUP - 1] - (GROUP - 1)
            for part in range(GROUP - 2, -1, -1):
                start = jnp.where(sub < (part + 1) * span_len, order[half, 1, GROUP * index + part] - part, start)
            key_pos = start * span_len + sub
            scores = lax.dot_general(
                key_list[rows], q_cat[...], (((1,), (1,)), ((), ())), preferred_element_type=F32
            )
            allowed = (key_pos <= query_pos) & (key_pos >= doc_first)
            scores = jnp.where(allowed, scores, NEG_LARGE)
            score_buf[index] = scores
            dprob_buf[index] = lax.dot_general(
                value_list[rows], g_cat[...], (((1,), (1,)), ((), ())), preferred_element_type=F32
            )
            return jnp.maximum(top, jnp.max(scores, axis=0, keepdims=True))

        top = lax.fori_loop(0, steps, score_step, jnp.full((1, lanes), NEG_LARGE, F32))

        def exp_step(index, sums):
            total, weighted = sums
            expd = jnp.exp((score_buf[index] - top) * scale)
            score_buf[index] = expd
            return (
                total + jnp.sum(expd, axis=0, keepdims=True),
                weighted + jnp.sum(expd * dprob_buf[index], axis=0, keepdims=True),
            )

        zero_row = jnp.zeros((1, lanes), F32)
        total, weighted = lax.fori_loop(0, steps, exp_step, (zero_row, zero_row))
        inverse = 1.0 / total
        delta = weighted * inverse
        dq_acc[...] = jnp.zeros_like(dq_acc)

        def grad_step(index, ds_now):
            rows = pl.ds(pl.multiple_of(index * GROUP * span_len, span_len), GROUP * span_len)
            probs = score_buf[index] * inverse
            dscores = probs * (dprob_buf[index] - delta)
            probs_low = probs.astype(BF16)
            ds_low = dscores.astype(BF16)
            grad_v = jnp.dot(probs_low, g_cat[...], preferred_element_type=F32)
            grad_k = jnp.dot(ds_low, q_cat[...], preferred_element_type=F32)
            for part in range(GROUP):
                block = pl.ds(pl.multiple_of(order[half, 0, GROUP * index + part] * span_len, span_len), span_len)
                own_part = slice(part * span_len, (part + 1) * span_len)
                dv_acc[block] += grad_v[own_part]
                dk_acc[block] += grad_k[own_part]
            dq_acc[...] += lax.dot_general(
                key_list[rows], ds_low, (((0,), (0,)), ((), ())), preferred_element_type=F32
            )
            return jnp.maximum(ds_now, jnp.max(jnp.abs(dscores), axis=0, keepdims=True))

        ds_top = lax.fori_loop(0, steps, grad_step, ds_top)
        cosine = rope[half, :, :head_dim]
        signed_sine = rope[half, :, head_dim:]
        grad_q = dq_acc[...].T * scale
        for head in range(heads):
            part = grad_q[head * span_len : (head + 1) * span_len]
            gq_ref[own, pl.ds(head * head_dim, head_dim)] = unrotate(part, cosine, signed_sine).astype(BF16)

    extra = spread_max(jnp.max(out_top[...]), jnp.max(ds_top), 2 * head_dim)
    for index in range(shards):
        rows = pl.ds(pl.multiple_of((me ^ index) * tok_dev, tok_dev), tok_dev)
        target = (keep_ref, send_ref)[index % 2]
        kind = target.dtype
        target[index // 2, :tok_dev, :head_dim] = dk_acc[rows].astype(kind)
        target[index // 2, :tok_dev, head_dim:] = dv_acc[rows].astype(kind)
        target[index // 2, tok_dev:] = extra.astype(kind)


def merge_kernel(keep_ref, got_ref, next_ref, send_ref):
    tok_dev = keep_ref.shape[1] - EXTRA
    extra = join_max([keep_ref[0, tok_dev:], got_ref[0, tok_dev:]])
    for index in range(keep_ref.shape[0]):
        both = keep_ref[index, :tok_dev] + got_ref[index, :tok_dev].astype(F32)
        target = (next_ref, send_ref)[index % 2]
        target[index // 2, :tok_dev] = both.astype(target.dtype)
        target[index // 2, tok_dev:] = extra.astype(target.dtype)


def finish_kernel(rope, gq_ref, keep_ref, got_ref, rows_ref, gkv_ref):
    tok_dev, width = gq_ref.shape
    head_dim = keep_ref.shape[2] // 2
    total = keep_ref[0, :tok_dev] + got_ref[0, :tok_dev].astype(F32)
    extra = join_max([keep_ref[0, tok_dev:], got_ref[0, tok_dev:]])
    wide = rope[...].reshape(tok_dev, 2 * head_dim)
    grad_k = unrotate(
        total[:, :head_dim] * (1.0 / math.sqrt(head_dim)), wide[:, :head_dim], wide[:, head_dim:]
    ).astype(BF16)
    grad_v = total[:, head_dim:].astype(BF16)
    gkv_ref[:tok_dev, :head_dim] = grad_k
    gkv_ref[:tok_dev, head_dim:] = grad_v
    gkv_ref[tok_dev:] = extra.astype(BF16)
    rows_ref[:, :width] = gq_ref[...]
    rows_ref[:, width : width + head_dim] = grad_k
    rows_ref[:, width + head_dim :] = grad_v


def partial_kernel(count, groups, blocks, tile, adds, *refs):
    xs, gs = refs[: groups * count], refs[groups * count : (groups + 1) * count]
    rest = refs[(groups + 1) * count :]
    tok_dev = xs[0].shape[0]
    for index in range(blocks * groups):
        block, group = index // groups, index % groups
        cols = slice(block * tile, (block + 1) * tile)
        total = None
        for x_ref, g_ref in zip(xs[group * count : (group + 1) * count], gs):
            term = lax.dot_general(
                x_ref[:, cols], g_ref[:tok_dev], (((0,), (0,)), ((), ())), preferred_element_type=F32
            )
            total = term if total is None else total + term
        rows = slice(index * tile, (index + 1) * tile)
        if adds:
            total = total + rest[0][rows].astype(F32)
            target = rest[1 + block % 2]
            place = block // 2 * groups + group
            target[place * tile : (place + 1) * tile] = total.astype(target.dtype)
        else:
            rest[0][rows] = total.astype(BF16)


def total_kernel(places, *refs):
    out_ref, amax_ref = refs[-2:]
    used = 0
    for (rows, cols), count in places:
        total = refs[used][: rows.stop - rows.start]
        for ref in refs[used + 1 : used + count]:
            total = total + ref[: rows.stop - rows.start].astype(F32)
        out_ref[rows, cols] = total
        used += count
    maxima = [ref[ref.shape[0] - EXTRA :] for ref in refs[used:-2]]
    out_max, ds_max = read_max(join_max(maxima))
    lane = lax.broadcasted_iota(jnp.int32, (1, 2), 1)
    amax_ref[0] = jnp.where(lane == 0, out_max[:, :2], ds_max[:, :2])


def start_packing(replicas, shards, order, rest, refs, sems):
    rep, me = lax.axis_index("dp"), lax.axis_index("context")
    places = [(1, place, place - shards // 2) for place in range(shards // 2, shards)]
    if not rest:
        places = [(0, place, place) for place in range(shards)]
        places += [(1, place, shards + place) for place in range(shards // 2)]
    tile = refs[1].shape[1] // len(places)
    copies = []
    for step in range(replicas):
        for index, (part, place, spot) in enumerate(places):
            source = ((((rep ^ step) * shards) + (me ^ order[place])) * 2 + part) * tile
            copy = pltpu.make_async_copy(
                refs[0].at[:, pl.ds(pl.multiple_of(source, tile), tile)],
                refs[1 + step].at[:, pl.ds(spot * tile, tile)],
                sems.at[step, index],
            )
            copy.start()
            copies.append(copy)
    return copies


def pack_rest_kernel(replicas, shards, order, *refs):
    for copy in start_packing(replicas, shards, order, True, refs[:-1], refs[-1]):
        copy.wait()


def prepare_kernel(replicas, shards, order, pair_ref, docs_ref, k_ref, v_ref, table_ref, q_ref, g_ref, *refs):
    rope_sems, sems, x_sems, q_buf, g_buf = refs[-5:]
    x_refs, outs = refs[:-12], refs[-12:-5]
    list_ref, kv_ref, bounds_ref, top_ref, rope_ref, q_cat, g_cat = outs
    x_copies = []
    if x_refs:
        x_copies = start_packing(replicas, shards, order, False, x_refs, x_sems)
    kv_ref[:, : k_ref.shape[1]] = k_ref[...]
    kv_ref[:, k_ref.shape[1] :] = v_ref[...]
    waits = [pltpu.make_async_copy(q_ref, q_buf, sems.at[0]), pltpu.make_async_copy(g_ref, g_buf, sems.at[1])]
    for copy in waits:
        copy.start()
    tok_dev = q_ref.shape[0]
    span_len = tok_dev // 2
    lanes, head_dim = q_cat.shape[1:]
    me = lax.axis_index("context")
    pair = pair_ref[me]
    copies = []
    for half in range(2):
        start = pl.multiple_of(span_of(pair, half, shards) * span_len, 8)
        copy = pltpu.make_async_copy(table_ref.at[pl.ds(start, span_len)], rope_ref.at[half], rope_sems.at[half])
        copy.start()
        copies.append(copy)
    docs = docs_ref[...]
    starts = [jnp.sum(jnp.where(docs < value, 1.0, 0.0)) for value in range(1, DOC_VALUES)]
    lane_row = lax.broadcasted_iota(jnp.int32, (1, lanes), 1) % span_len
    for half in range(2):
        span = span_of(pair, half, shards)
        base = span * span_len
        base_f = base.astype(F32)
        first_start = jnp.float32(0.0)
        for start in starts:
            first_start = jnp.maximum(first_start, jnp.where(start <= base_f, start, 0.0))
        first_key = first_start.astype(jnp.int32)

        def listing(block, count):
            other = pair_ref[block // 2]
            key_span = jnp.where(block % 2 == 0, other, 2 * shards - 1 - other)
            list_ref[half, 0, count] = block
            list_ref[half, 1, count] = key_span
            needed = (key_span <= span) & (key_span * span_len + span_len > first_key)
            return count + needed.astype(jnp.int32)

        count = lax.fori_loop(0, 2 * shards, listing, jnp.int32(0))
        list_ref[half, 2, 0] = count
        for spare in range(GROUP - 1):
            list_ref[half, 0, count + spare] = 2 * shards
            list_ref[half, 1, count + spare] = 2 * shards
        query_pos = base + lane_row
        query_f = query_pos.astype(F32)
        doc_start = jnp.zeros((1, lanes), F32)
        for start in starts:
            doc_start = jnp.maximum(doc_start, jnp.where(start <= query_f, start, 0.0))
        bounds_ref[half, 0:1] = doc_start.astype(jnp.int32)
        bounds_ref[half, 1:2] = query_pos
    waits[0].wait()
    waits[1].wait()
    for half in range(2):
        own = slice(half * span_len, (half + 1) * span_len)
        for head in range(q_ref.shape[1] // head_dim):
            rows = slice(head * span_len, (head + 1) * span_len)
            cols = slice(head * head_dim, (head + 1) * head_dim)
            q_cat[half, rows] = q_buf[own, cols]
            g_cat[half, rows] = g_buf[own, cols]
    top_ref[...] = jnp.max(jnp.abs(g_cat[...].astype(F32)).reshape(-1, 8, head_dim), axis=0)
    for copy in copies + x_copies:
        copy.wait()


def params(mebibytes):
    return pltpu.CompilerParams(vmem_limit_bytes=mebibytes << 20)


def cost(microseconds):
    return pl.CostEstimate(flops=int(microseconds * 1.0e6), bytes_accessed=0, transcendentals=0)


def local(query_rows, key_rows, value_rows, out_grads, layer_input, doc_ids, pair_span):
    shards = lax.axis_size("context")
    replicas = lax.axis_size("dp")
    tok_dev = query_rows.shape[1]
    head_dim = key_rows.shape[2]
    width = query_rows.shape[2]
    heads = width // head_dim
    model_width = layer_input.shape[2]
    span_len = tok_dev // 2
    seq_len = tok_dev * shards
    qkv_width = width + 2 * head_dim
    lanes = heads * span_len
    slice_rows = model_width // (replicas * shards)
    tile = slice_rows // 2
    packs = tile % 128 == 0
    half_shards = shards // 2
    table = jnp.asarray(rope_tables(seq_len, head_dim))
    order = list(range(1, shards, 2)) + list(range(0, shards, 2))

    def context_move(x, step):
        return lax.ppermute(x, "context", [(i, i ^ step) for i in range(shards)])

    def dp_move(x, step):
        return lax.ppermute(x, "dp", [(i, i ^ step) for i in range(replicas)])

    def struct(shape, kind=BF16):
        return jax.ShapeDtypeStruct(shape, kind)

    outs = [
        struct((2, 3, 2 * shards + GROUP), jnp.int32),
        struct((tok_dev, 2 * head_dim)),
        struct((2, 2, lanes), jnp.int32),
        struct((8, head_dim), F32),
        struct((2, span_len, 2 * head_dim), F32),
        struct((2, lanes, head_dim)),
        struct((2, lanes, head_dim)),
    ]
    if packs:
        outs = [struct((tok_dev, (shards + half_shards) * tile))] * replicas + outs
    prepared = pl.pallas_call(
        functools.partial(prepare_kernel, replicas, shards, order),
        out_shape=outs,
        in_specs=[SMEM] + [VMEM] * 3 + [ANY] * (3 + packs),
        out_specs=[VMEM] * (len(outs) - 7) + [SMEM] + [VMEM] * 6,
        scratch_shapes=[
            pltpu.SemaphoreType.DMA((2,)),
            pltpu.SemaphoreType.DMA((2,)),
            pltpu.SemaphoreType.DMA((replicas, shards + half_shards)),
            pltpu.VMEM((tok_dev, width), BF16),
            pltpu.VMEM((tok_dev, width), BF16),
        ],
        compiler_params=params(60),
        cost_estimate=cost(4),
        name="prepare",
    )(pair_span, doc_ids, key_rows[0], value_rows[0], table, query_rows[0], out_grads[0], *([layer_input[0]] if packs else []))
    order_list, own_kv, bounds, out_top, rope, q_cats, g_cats = prepared[-7:]
    if packs:
        x_most = list(prepared[:replicas])
    else:
        me, rep = lax.axis_index("context"), lax.axis_index("dp")
        x_most, x_rest = [], []
        for step in range(replicas):
            part = lax.dynamic_slice_in_dim(layer_input[0], (rep ^ step) * shards * slice_rows, shards * slice_rows, 1)
            part = jnp.take(part.reshape(tok_dev, shards, 2, tile), jnp.asarray(order, jnp.int32) ^ me, axis=1)
            most = jnp.concatenate([part[:, :, 0], part[:, :half_shards, 1]], axis=1)
            x_most.append(most.reshape(tok_dev, -1))
            x_rest.append(part[:, half_shards:, 1].reshape(tok_dev, -1))

    def tie(value, *others):
        return lax.optimization_barrier((value, others))[0]

    def exchange(parts):
        return [parts[0]] + [dp_move(parts[step], step) for step in range(1, replicas)]

    x_most = exchange(x_most)
    kv_all = lax.all_gather(own_kv, "context", axis=0, tiled=True)

    buf = ((2 * shards + GROUP - 1) // GROUP, GROUP * span_len, lanes)
    padded = (seq_len + GROUP * span_len, head_dim)
    grad_q, keep, send = pl.pallas_call(
        functools.partial(attend_kernel, shards, heads),
        out_shape=[
            struct((tok_dev, width)),
            struct((shards // 2, tok_dev + EXTRA, 2 * head_dim)),
            struct((shards // 2, tok_dev + EXTRA, 2 * head_dim)),
        ],
        in_specs=[SMEM] + [VMEM] * 6,
        out_specs=[VMEM] * 3,
        scratch_shapes=[
            pltpu.VMEM(padded, BF16),
            pltpu.VMEM(padded, BF16),
            pltpu.VMEM(buf, F32),
            pltpu.VMEM(buf, F32),
            pltpu.VMEM((head_dim, lanes), F32),
            pltpu.VMEM(padded, F32),
            pltpu.VMEM(padded, F32),
        ],
        compiler_params=params(60),
        cost_estimate=cost(12),
        name="attend",
    )(order_list, rope, bounds, out_top, q_cats, g_cats, kv_all)

    grad_q, send = tie((grad_q, send), x_most)
    gq = exchange([grad_q] * replicas)
    if packs:
        x_rest = pl.pallas_call(
            functools.partial(pack_rest_kernel, replicas, shards, order),
            out_shape=[struct((tok_dev, half_shards * tile))] * replicas,
            in_specs=[ANY],
            out_specs=[VMEM] * replicas,
            scratch_shapes=[pltpu.SemaphoreType.DMA((replicas, half_shards))],
            compiler_params=params(8),
            cost_estimate=cost(2),
            name="pack_rest",
        )(tie(layer_input[0], send))
        x_rest = list(x_rest)

    block = (tok_dev + EXTRA, 2 * head_dim)
    got, step = context_move(send, 1), 2
    while step < shards:
        count = shards // 2 // step
        keep, send = pl.pallas_call(
            merge_kernel,
            out_shape=[struct((count,) + block, F32), struct((count,) + block)],
            in_specs=[VMEM] * 2,
            out_specs=[VMEM] * 2,
            compiler_params=params(8),
        cost_estimate=cost(2),
            name="merge_rows",
        )(keep, got)
        got, step = context_move(send, step), step * 2

    def partial_weights(groups, gs, arrived=None):
        parts = [x for _, xs in groups for x in xs]
        block = (tok_dev, half_shards * tile)
        specs = [pl.BlockSpec(block, lambda i, first=first: (0, first)) for first, xs in groups for _ in xs]
        rows, cols = half_shards * len(groups) * tile, gs[0].shape[1]
        adds = arrived is not None
        out_shape = [struct((rows, cols))]
        if adds:
            out_shape = [struct((rows // 2, cols), F32), struct((rows // 2, cols))]
        result = pl.pallas_call(
            functools.partial(partial_kernel, replicas, len(groups), half_shards, tile, adds),
            out_shape=out_shape,
            grid=(1,),
            in_specs=specs + [VMEM] * (replicas + adds),
            out_specs=[VMEM] * len(out_shape),
            compiler_params=params(16),
            cost_estimate=cost(2),
            name="weights_own_core" if adds else "weights_other_core",
        )(*parts, *gs, *([arrived] if adds else []))
        return result if adds else result[0]

    def split_blocks(x, rows):
        parts = x.reshape(-1, 2, rows, x.shape[1])
        return parts[:, 0].reshape(-1, x.shape[1]), parts[:, 1].reshape(-1, x.shape[1])

    def next_terms(kept, got, rows):
        kept_even, kept_odd = split_blocks(kept, rows)
        got_even, got_odd = split_blocks(got, rows)
        return kept_even + got_even.astype(F32), (kept_odd + got_odd.astype(F32)).astype(BF16)

    def last_steps(kept, got, rows):
        terms, step, sent = [kept, got], 4, got
        while step < shards:
            kept, sent = next_terms(kept, got, rows)
            got, step = context_move(sent, step), step * 2
            terms.append(got)
        return terms, sent

    gq = tie(gq, keep, got, x_rest)
    away = partial_weights([(0, x_most)], gq)
    arrived = context_move(away, 1)
    keep, got = tie((keep, got), away)
    grad_rows, grad_kv = pl.pallas_call(
        finish_kernel,
        out_shape=[struct((tok_dev, qkv_width)), struct(block)],
        in_specs=[VMEM] * 4,
        out_specs=[VMEM] * 2,
        compiler_params=params(8),
        cost_estimate=cost(2),
        name="finish_rows",
    )(rope, grad_q, keep, got)
    x_rest = exchange(tie(x_rest, gq))
    gkv = exchange([grad_kv] * replicas)
    away = partial_weights([(2, tie(x_most, away))], gq)
    kept, sent = partial_weights([(1, x_most)], gq, tie(arrived, grad_kv, away))
    first = kept, context_move(sent, 2)
    arrived = context_move(away, 1)
    first, sent = last_steps(*first, tile)
    kept, sent = partial_weights([(0, x_rest)], gq, tie(arrived, sent))
    second = kept, context_move(sent, 2)
    away = partial_weights([(0, x_most), (2, x_most)], tie(gkv, sent, first))
    arrived = context_move(away, 1)
    second, sent = last_steps(*second, tile)
    kept, sent = partial_weights([(1, x_most), (0, x_rest)], gkv, tie(arrived, sent))
    third = last_steps(kept, context_move(sent, 2), 2 * tile)[0]
    terms = [first, second, third]
    upper, lower, full = slice(0, tile), slice(tile, 2 * tile), slice(0, width)
    spots = [(upper, full), (lower, full), (slice(0, 2 * tile), slice(width, qkv_width))]
    places = [(spot, len(part)) for spot, part in zip(spots, terms)]
    grad_weight, amax = pl.pallas_call(
        functools.partial(total_kernel, places),
        out_shape=[struct((slice_rows, qkv_width), F32), struct((1, 1, 2), F32)],
        in_specs=[VMEM] * (sum(len(part) for part in terms) + replicas),
        out_specs=[VMEM] * 2,
        compiler_params=params(16),
        name="total_weights",
    )(*[x for part in terms for x in part], *gkv)
    return (grad_rows[None], grad_weight, amax)


def solution(mesh):
    in_specs = (
        P("dp", "context", None),
        P("dp", "context", None),
        P("dp", "context", None),
        P("dp", "context", None),
        P("dp", "context", None),
        P("dp", None),
        P(),
    )
    out_specs = (P("dp", "context", None), P(("dp", "context"), None), P("dp", "context", None))
    return jax.shard_map(local, mesh=mesh, in_specs=in_specs, out_specs=out_specs, check_vma=False)
```
